256 devices in a mesh: dp: 4 (over y_lo, core), fsdp: 64 (over y_hi, x, z).
Axes of the slice: x: 4, y: 4 (y_hi: 2, y_lo: 2; y = y_hi * 2 + y_lo), z: 8, core: 2. Of those that a mesh axis runs over, the one named last changes fastest.
Arguments:
- acts: bfloat16 [4, 32768, 4096], P('dp', 'fsdp')
- token_ids: int32 [4, 32768], P('dp', 'fsdp'), may hold values from 127232 to 128255
- turn_ids: int32 [4, 32768], P('dp', 'fsdp'), may hold values from 0 to 255, never falling along the last dimension, each value on 1 to 512 neighbouring positions
- value_weight: bfloat16 [4096, 512], P('fsdp'), may hold values from -0.09375 to 0.09375
- norm_gain: float32 [512], replicated, may hold values from 0.5 to 1.5
- query_grad: float32 [4096, 512], P('fsdp'), may hold values from -6 to 6
Outputs:
- estimate: float32 [4096, 512], P('fsdp')
The draws below stay inside these ranges and needn't reach their ends.
All inputs are finite; a program needn't handle non-finite values.
Results may differ from the reference program's by a relative error of at most 0.0032.
Values may be sent and summed in bfloat16 or wider, within the bound.
No kernel may reach another device: no remote copies, remote signals or barrier semaphores. Data moves between devices by JAX's collectives and lax.ppermute only.
A program may use at most 64 MiB of HBM per device.

```python
import math
import jax
import jax.numpy as jnp
import numpy as np
from jax import lax

DIN = 4096
KV = 512
ITERS = 2
GROUP_TOK = 32768
TURNS = 256
TURN_MOST = 512
N_DP = 4


def draw_acts(key, part):
    key = jax.random.fold_in(key, 11)
    key_col, key_row, key_main = jax.random.split(key, 3)
    column = jnp.exp(jax.random.uniform(key_col, (DIN,), jnp.float32, jnp.log(0.5), jnp.log(2.0)))
    row = jnp.exp(jax.random.uniform(key_row, (N_DP, GROUP_TOK, 1), jnp.float32, jnp.log(0.3), jnp.log(3.0)))
    main = jax.random.normal(key_main, (N_DP, GROUP_TOK, DIN), jnp.float32)
    result = main * row * column
    return result.astype(jnp.bfloat16)


def plant(array, key, least, largest):
    dims = array.shape
    index_at = [jax.random.randint(jax.random.fold_in(key, axis), (), 0, dims[axis]) for axis in range(len(dims))]
    array = array.at[tuple(index_at)].set(least)
    longest = dims.index(max(dims))
    index_at[longest] = (index_at[longest] + 1) % dims[longest]
    return array.at[tuple(index_at)].set(largest)


def block_scale(stream_key, shape, pieces, low, high):
    def one(position, shards_of):
        heights = jax.random.uniform(jax.random.fold_in(jax.random.fold_in(stream_key, 6), position), (shards_of,), jnp.float32, low / len(pieces), high / len(pieces))
        return jnp.repeat(jnp.exp(heights), shape[position] // shards_of).reshape((-1,) + (1,) * (len(shape) - position - 1))

    level = one(*pieces[0])
    for cut in pieces[1:]:
        level = level * one(*cut)
    return level


def split_up(amount, total, most, slope):
    portions = [(1 << 20) // math.isqrt(rank ** slope) + 1 for rank in range(2, amount + 1)]
    rest, given = total - most - (amount - 1), [1] * (amount - 1)
    while rest > 0:
        free = [i for i in range(amount - 1) if given[i] < most]
        whole, left = sum([portions[i] for i in free]), rest
        for i in free:
            extra = min(most - given[i], max(1, left * portions[i] // whole), rest)
            given[i] = given[i] + extra
            rest = rest - extra
    return np.array([most] + given)


def uneven_parts(stream_key, count, total, limit, skew):
    if count == 2:
        one = jax.random.randint(stream_key, (), max(1, total - limit), min(limit, total - 1) + 1)
        return jnp.stack([one, total - one])
    lengths = jnp.asarray(split_up(count, total, limit, skew), jnp.int32)
    couples = (count - 1) // 2
    giver, taker = lengths[1:1 + 2 * couples:2], lengths[2:2 + 2 * couples:2]
    room = jnp.minimum(giver - 1, limit - taker)
    shifted = jax.random.randint(jax.random.fold_in(stream_key, 1), (couples,), 0, 1 << 20) % (room + 1)
    lengths = lengths.at[1:1 + 2 * couples:2].set(giver - shifted).at[2:2 + 2 * couples:2].set(taker + shifted)
    return lengths[jax.random.permutation(jax.random.fold_in(stream_key, 2), count)]


def normal_values(stream_key, shape, width, reach, cuts=(), held_as=jnp.bfloat16):
    gain = block_scale(stream_key, shape, cuts, -0.22, 0.18) if cuts else 1.0
    drawn = jax.random.normal(stream_key, shape, jnp.float32) * width * gain
    return jnp.minimum(jnp.maximum(drawn, -reach), reach).astype(held_as)


def setup_inputs(seed: int = 0) -> dict:
    seeds = jax.random.split(jax.random.key(seed), 7)
    acts = draw_acts(jax.random.fold_in(seeds[6], 71), 0)
    token_ids = plant(jax.random.randint(seeds[1], (N_DP, GROUP_TOK), 127232, 128256), jax.random.fold_in(seeds[1], 1), 127232, 128255).astype(jnp.int32)
    turn_ids = jax.vmap(lambda own: jnp.searchsorted(jnp.cumsum(uneven_parts(own, TURNS, GROUP_TOK, TURN_MOST, 2)), jnp.arange(GROUP_TOK), side="right"))(jax.random.split(seeds[2], N_DP)).reshape((N_DP, GROUP_TOK)).astype(jnp.int32)
    value_weight = normal_values(seeds[3], (DIN, KV), DIN ** -0.5, 0.09375, ((0, 64),))
    norm_gain = jnp.clip(jnp.exp(jax.random.uniform(seeds[4], (KV,), jnp.float32, math.log(0.5), math.log(1.5))), 0.5, 1.5)
    query_grad = normal_values(seeds[5], (DIN, KV), 1.0, 6.0, ((0, 64),), jnp.float32)
    return {"acts": acts, "token_ids": token_ids, "turn_ids": turn_ids, "value_weight": value_weight, "norm_gain": norm_gain, "query_grad": query_grad}


damping = 1.0
lissa_scale = 12.0
first_special = 128000

def norm_jacobian(vector, unit_values, root_mean):
    inner = lax.optimization_barrier(jnp.mean(unit_values * vector, axis=-1, keepdims=True))
    return (vector - unit_values * inner) / root_mean

def reference(acts, token_ids, turn_ids, value_weight, norm_gain, query_grad):
    gain_square = norm_gain * norm_gain
    turn_total = jnp.float32(TURNS * N_DP)
    groups = []
    for group in range(N_DP):
        inputs = acts[group]
        text_mask = (token_ids[group] < first_special).astype(jnp.float32)
        counts = jax.ops.segment_sum(text_mask, turn_ids[group], num_segments=TURNS)
        turn_weight = text_mask / (jnp.maximum(counts[turn_ids[group]], 1.0) * turn_total)
        values = jnp.dot(inputs, value_weight, preferred_element_type=jnp.float32)
        root_mean = jnp.sqrt(lax.optimization_barrier(jnp.mean(values * values, axis=-1, keepdims=True)) + 1e-06)
        groups.append((inputs, turn_weight, values / root_mean, root_mean))
    estimate = query_grad
    for step in range(ITERS):
        sent_rows = estimate.astype(jnp.bfloat16)
        curvature = jnp.zeros(query_grad.shape, jnp.float32)
        for inputs, turn_weight, unit_values, root_mean in groups:
            tangent = jnp.dot(inputs, sent_rows, preferred_element_type=jnp.float32)
            inner = gain_square * norm_jacobian(tangent, unit_values, root_mean)
            adjoint = (turn_weight[:, None] * norm_jacobian(inner, unit_values, root_mean)).astype(jnp.bfloat16)
            curvature = curvature + lax.dot_general(inputs, adjoint, (((0,), (0,)), ((), ())), preferred_element_type=jnp.float32)
        estimate = query_grad + estimate - (curvature + damping * estimate) / lissa_scale
    return estimate
```

```python
import jax
import jax.numpy as jnp
from jax import lax
from jax.sharding import Mesh, PartitionSpec as P

TURN_DEV = 4
ITERS = 2

damping = 1.0
lissa_scale = 12.0
first_special = 128000

FINE = ("ylo", "core", "yhi", "x", "z")
GROUP = ("ylo", "core")
SHARD = ("yhi", "x", "z")
PLANE = ("x", "z")
RING = ("ylo", "yhi")


def ring_place():
    return lax.axis_index("yhi") * 2 + lax.axis_index("ylo")


def ring_shift(value, step):
    def number(y):
        return (y % 2) * 2 + y // 2

    return lax.ppermute(value, RING, [(number(y), number((y + step) % 4)) for y in range(4)])


def core_swap(value):
    return lax.ppermute(value, "core", [(0, 1), (1, 0)])


def ring_gather(block, rows, cols):
    me = ring_place()
    half = rows // 2
    before = ring_shift(block, 1)
    after = ring_shift(block, -1)
    far_top = ring_shift(after[:half], -1)
    far_low = ring_shift(before[half:], 1)
    whole = jnp.zeros((2 * rows, 2 * cols), block.dtype)

    def put(whole, piece, step, start):
        at = (me + step) % 4
        return lax.dynamic_update_slice(whole, piece, ((at // 2) * rows + start, (at % 2) * cols))

    whole = put(whole, block, 0, 0)
    whole = put(whole, before, 3, 0)
    whole = put(whole, after, 1, 0)
    whole = put(whole, far_top, 2, 0)
    return put(whole, far_low, 2, half)


def ring_scatter(whole):
    me = ring_place()
    rows, cols = whole.shape[0] // 2, whole.shape[1] // 2
    half = rows // 2

    def take(step, start, size):
        at = (me + step) % 4
        return lax.dynamic_slice(
            whole, ((at // 2) * rows + start, (at % 2) * cols), (size, cols)
        )

    sent = jnp.bfloat16
    top = ring_shift(take(2, 0, half).astype(sent), 1)
    low = ring_shift(take(2, half, half).astype(sent), -1)
    up = jnp.concatenate(
        [take(1, 0, half) + top.astype(jnp.float32), take(1, half, half)], axis=0
    ).astype(sent)
    down = jnp.concatenate(
        [take(3, 0, half), take(3, half, half) + low.astype(jnp.float32)], axis=0
    ).astype(sent)
    from_before = ring_shift(up, 1).astype(jnp.float32)
    from_after = ring_shift(down, -1).astype(jnp.float32)
    return take(0, 0, rows) + from_before + from_after


def spread(block, axes):
    n = lax.axis_size(axes)
    copies = jnp.broadcast_to(block[None], (n,) + block.shape)
    return lax.all_to_all(copies, axes, split_axis=0, concat_axis=0, tiled=True)


def gather_halves(block):
    rows, cols = block.shape
    plane = spread(block, PLANE)
    n = plane.shape[0]
    mine = ring_gather(plane.reshape(n * rows, cols), n * rows, cols)
    return mine, core_swap(mine)


def reduce_blocks(inputs, adjoint):
    half = adjoint.shape[1] // 2

    def outer(part):
        return lax.dot_general(
            inputs, part, (((0,), (0,)), ((), ())), preferred_element_type=jnp.float32
        )

    other = core_swap(outer(adjoint[:, half:]).astype(jnp.bfloat16))
    chip = outer(adjoint[:, :half]) + other.astype(jnp.float32)
    column = ring_scatter(chip).astype(jnp.bfloat16)
    n = lax.axis_size(PLANE)
    parts = lax.all_to_all(
        column.reshape((n, column.shape[0] // n, column.shape[1])),
        PLANE,
        split_axis=0,
        concat_axis=0,
        tiled=True,
    )
    return jnp.sum(parts.astype(jnp.float32), axis=0)


def norm_jacobian(vector, unit_values, root_mean):
    inner = jnp.mean(unit_values * vector, axis=-1, keepdims=True)
    return (vector - unit_values * inner) / root_mean


def turn_counts(text_mask, turn_ids):
    n = lax.axis_size(SHARD)
    first, last = turn_ids[0], turn_ids[-1]

    def edge(turn):
        count = jnp.sum(jnp.where(turn_ids == turn, text_mask, 0.0))
        row = jnp.stack([turn.astype(jnp.float32), count])
        return jnp.broadcast_to(row[:, None, None], (2, 8, 128))

    left = lax.ppermute(edge(last), SHARD, [(i, i + 1) for i in range(n - 1)])
    right = lax.ppermute(edge(first), SHARD, [(i + 1, i) for i in range(n - 1)])
    same = turn_ids[:, None] == turn_ids[None, :]
    counts = jnp.sum(jnp.where(same, text_mask[None, :], 0.0), axis=1)
    as_float = turn_ids.astype(jnp.float32)
    for other in (left, right):
        counts = counts + jnp.where(as_float == other[0, 0, 0], other[1, 0, 0], 0.0)
    return counts


def local(acts, token_ids, turn_ids, value_weight, norm_gain, query_grad):
    inputs = acts.reshape(acts.shape[1], acts.shape[2])
    ids = turn_ids.reshape(-1)
    features = value_weight.shape[1]
    n_group = lax.axis_size(GROUP)
    turn_total = TURN_DEV * lax.axis_size(SHARD) * n_group
    cols = features // n_group
    me = lax.axis_index(GROUP)
    core = lax.axis_index("core")
    text_mask = (token_ids.reshape(-1) < first_special).astype(jnp.float32)

    def own(array):
        return lax.dynamic_slice(array, (0, me * cols), (array.shape[0], cols))

    def project(halves):
        return jnp.concatenate(
            [jnp.dot(inputs, half, preferred_element_type=jnp.float32) for half in halves], axis=1
        )

    gain = norm_gain.reshape(2, 2, cols)
    gain = jnp.concatenate(
        [jnp.where(core == 0, gain[:, 0], gain[:, 1]), jnp.where(core == 0, gain[:, 1], gain[:, 0])]
    ).reshape(-1)
    gain_square = gain * gain
    query = own(query_grad)

    values = project(gather_halves(own(value_weight)))
    tangent = project(gather_halves(query.astype(jnp.bfloat16)))
    own_count = turn_counts(text_mask, ids)
    turn_weight = text_mask / (jnp.maximum(own_count, 1.0) * jnp.float32(turn_total))
    root_mean = jnp.sqrt(jnp.mean(values * values, axis=-1, keepdims=True) + 1e-06)
    unit_values = values / root_mean
    estimate = query
    for step in range(ITERS):
        if step:
            tangent = project(gather_halves(estimate.astype(jnp.bfloat16)))
        inner = gain_square * norm_jacobian(tangent, unit_values, root_mean)
        adjoint = (turn_weight[:, None] * norm_jacobian(inner, unit_values, root_mean)).astype(
            jnp.bfloat16
        )
        curvature = reduce_blocks(inputs, adjoint)
        estimate = query + estimate - (curvature + damping * estimate) / lissa_scale
    whole = spread(estimate, GROUP)
    return jnp.concatenate([whole[i] for i in range(n_group)], axis=1)


def solution(mesh):
    fine = Mesh(mesh.devices.reshape(2, 2, 2, 4, 8), FINE)
    placed = (
        P(GROUP, SHARD, None),
        P(GROUP, SHARD),
        P(GROUP, SHARD),
        P(SHARD, None),
        P(),
        P(SHARD, None),
    )
    return jax.shard_map(
        local, mesh=fine, in_specs=placed, out_specs=P(SHARD, None), check_vma=False
    )
```

```python
import jax
import jax.numpy as jnp
from jax import lax
from jax.sharding import Mesh, PartitionSpec as P

TURN_DEV = 4
ITERS = 2

damping = 1.0
lissa_scale = 12.0
first_special = 128000

FINE = ("ylo", "core", "yhi", "x", "z")
GROUP = ("ylo", "core")
SHARD = ("yhi", "x", "z")
PLANE = ("ylo", "yhi", "x")


def core_swap(value):
    return lax.ppermute(value, "core", [(0, 1), (1, 0)])


def exchange(blocks, axes):
    return lax.all_to_all(blocks, axes, split_axis=0, concat_axis=0, tiled=True)


def spread(block, axes):
    n = lax.axis_size(axes)
    return exchange(jnp.broadcast_to(block[None], (n,) + block.shape), axes)


def gather_plane(block):
    plane = spread(block, PLANE)
    n = lax.axis_size("ylo")
    plane = plane.reshape(n, plane.shape[0] // n * plane.shape[1], plane.shape[2])
    mine = jnp.concatenate([plane[i] for i in range(n)], axis=1)
    return mine, core_swap(mine)


def gather_line(block):
    line = spread(block, "z")
    return line.reshape(line.shape[0] * line.shape[1], line.shape[2])


def reduce_blocks(inputs, adjoint):
    half = adjoint.shape[1] // 2

    def outer(part):
        return lax.dot_general(
            inputs, part, (((0,), (0,)), ((), ())), preferred_element_type=jnp.float32
        )

    other = core_swap(outer(adjoint[:, half:]).astype(jnp.bfloat16))
    chip = outer(adjoint[:, :half]) + other.astype(jnp.float32)
    n_low, n_plane, n_line = lax.axis_size("ylo"), lax.axis_size(PLANE), lax.axis_size("z")
    cols = half // n_low
    columns = jnp.stack([chip[:, i * cols : (i + 1) * cols] for i in range(n_low)])
    columns = columns.astype(jnp.bfloat16).reshape(n_plane, -1, cols)
    line = jnp.sum(exchange(columns, PLANE).astype(jnp.float32), axis=0)
    line = line.astype(jnp.bfloat16).reshape(n_line, -1, cols)
    return jnp.sum(exchange(line, "z").astype(jnp.float32), axis=0)


def norm_jacobian(vector, unit_values, root_mean):
    inner = jnp.mean(unit_values * vector, axis=-1, keepdims=True)
    return (vector - unit_values * inner) / root_mean


def turn_counts(text_mask, turn_ids):
    n = lax.axis_size(SHARD)
    first, last = turn_ids[0], turn_ids[-1]

    def edge(turn):
        count = jnp.sum(jnp.where(turn_ids == turn, text_mask, 0.0))
        row = jnp.stack([turn.astype(jnp.float32), count])
        return jnp.broadcast_to(row[:, None, None], (2, 8, 128))

    left = lax.ppermute(edge(last), SHARD, [(i, i + 1) for i in range(n - 1)])
    right = lax.ppermute(edge(first), SHARD, [(i + 1, i) for i in range(n - 1)])
    same = turn_ids[:, None] == turn_ids[None, :]
    counts = jnp.sum(jnp.where(same, text_mask[None, :], 0.0), axis=1)
    as_float = turn_ids.astype(jnp.float32)
    for other in (left, right):
        counts = counts + jnp.where(as_float == other[0, 0, 0], other[1, 0, 0], 0.0)
    return counts


def local(acts, token_ids, turn_ids, value_weight, norm_gain, query_grad):
    inputs = acts.reshape(acts.shape[1], acts.shape[2])
    ids = turn_ids.reshape(-1)
    features = value_weight.shape[1]
    n_group = lax.axis_size(GROUP)
    turn_total = TURN_DEV * lax.axis_size(SHARD) * n_group
    cols = features // n_group
    me = lax.axis_index(GROUP)
    core = lax.axis_index("core")
    text_mask = (token_ids.reshape(-1) < first_special).astype(jnp.float32)

    def own(array):
        return lax.dynamic_slice(array, (0, me * cols), (array.shape[0], cols))

    def project(halves):
        return jnp.concatenate(
            [jnp.dot(inputs, half, preferred_element_type=jnp.float32) for half in halves], axis=1
        )

    gain = norm_gain.reshape(2, 2, cols)
    gain = jnp.concatenate(
        [jnp.where(core == 0, gain[:, 0], gain[:, 1]), jnp.where(core == 0, gain[:, 1], gain[:, 0])]
    ).reshape(-1)
    gain_square = gain * gain
    query = own(query_grad)

    both = gather_line(jnp.concatenate([own(value_weight), query.astype(jnp.bfloat16)], axis=1))
    values = project(gather_plane(both[:, :cols]))
    tangent = project(gather_plane(both[:, cols:]))
    own_count = turn_counts(text_mask, ids)
    turn_weight = text_mask / (jnp.maximum(own_count, 1.0) * jnp.float32(turn_total))
    root_mean = jnp.sqrt(jnp.mean(values * values, axis=-1, keepdims=True) + 1e-06)
    unit_values = values / root_mean
    estimate = query
    for step in range(ITERS):
        if step:
            tangent = project(gather_plane(gather_line(estimate.astype(jnp.bfloat16))))
        inner = gain_square * norm_jacobian(tangent, unit_values, root_mean)
        adjoint = (turn_weight[:, None] * norm_jacobian(inner, unit_values, root_mean)).astype(
            jnp.bfloat16
        )
        curvature = reduce_blocks(inputs, adjoint)
        estimate = query + estimate - (curvature + damping * estimate) / lissa_scale
    whole = spread(estimate, GROUP)
    return jnp.concatenate([whole[i] for i in range(n_group)], axis=1)


def solution(mesh):
    fine = Mesh(mesh.devices.reshape(2, 2, 2, 4, 8), FINE)
    placed = (
        P(GROUP, SHARD, None),
        P(GROUP, SHARD),
        P(GROUP, SHARD),
        P(SHARD, None),
        P(),
        P(SHARD, None),
    )
    return jax.shard_map(
        local, mesh=fine, in_specs=placed, out_specs=P(SHARD, None), check_vma=False
    )
```

```python
import jax
import jax.numpy as jnp
from jax import lax
from jax.sharding import Mesh, PartitionSpec as P

TURN_DEV = 4
ITERS = 2

damping = 1.0
lissa_scale = 12.0
first_special = 128000

FINE = ("ylo", "core", "yhi", "x", "z")
GROUP = ("ylo", "core")
SHARD = ("yhi", "x", "z")
LINE = ("ylo", "yhi", "z")


def core_swap(value):
    return lax.ppermute(value, "core", [(0, 1), (1, 0)])


def exchange(blocks, axes):
    return lax.all_to_all(blocks, axes, split_axis=0, concat_axis=0, tiled=True)


def spread(block, axes):
    n = lax.axis_size(axes)
    return exchange(jnp.broadcast_to(block[None], (n,) + block.shape), axes)


def gather_line(block):
    n = lax.axis_size("ylo")
    line = spread(block, LINE)
    line = line.reshape(n, line.shape[0] // n * line.shape[1], line.shape[2])
    return [line[i] for i in range(n)]


def gather_rows(pieces):
    rows = spread(jnp.concatenate(pieces, axis=1), "x")
    mine = rows.reshape(rows.shape[0] * rows.shape[1], rows.shape[2])
    return mine, core_swap(mine)


def reduce_blocks(inputs, adjoint):
    half = adjoint.shape[1] // 2

    def outer(part):
        return lax.dot_general(
            inputs, part, (((0,), (0,)), ((), ())), preferred_element_type=jnp.float32
        )

    other = core_swap(outer(adjoint[:, half:]).astype(jnp.bfloat16))
    chip = outer(adjoint[:, :half]) + other.astype(jnp.float32)
    n_low, n_line, n_x = lax.axis_size("ylo"), lax.axis_size(LINE), lax.axis_size("x")
    cols = half // n_low
    rows = chip.astype(jnp.bfloat16).reshape(n_x, -1, half)
    line = jnp.sum(exchange(rows, "x").astype(jnp.float32), axis=0).astype(jnp.bfloat16)
    line = jnp.concatenate([line[:, i * cols : (i + 1) * cols] for i in range(n_low)], axis=0)
    parts = exchange(line.reshape(n_line, -1, cols), LINE)
    return jnp.sum(parts.astype(jnp.float32), axis=0)


def norm_jacobian(vector, unit_values, root_mean):
    inner = jnp.mean(unit_values * vector, axis=-1, keepdims=True)
    return (vector - unit_values * inner) / root_mean


def turn_counts(text_mask, turn_ids):
    n = lax.axis_size(SHARD)
    first, last = turn_ids[0], turn_ids[-1]

    def edge(turn):
        count = jnp.sum(jnp.where(turn_ids == turn, text_mask, 0.0))
        row = jnp.stack([turn.astype(jnp.float32), count])
        return jnp.broadcast_to(row[:, None, None], (2, 8, 128))

    left = lax.ppermute(edge(last), SHARD, [(i, i + 1) for i in range(n - 1)])
    right = lax.ppermute(edge(first), SHARD, [(i + 1, i) for i in range(n - 1)])
    same = turn_ids[:, None] == turn_ids[None, :]
    counts = jnp.sum(jnp.where(same, text_mask[None, :], 0.0), axis=1)
    as_float = turn_ids.astype(jnp.float32)
    for other in (left, right):
        counts = counts + jnp.where(as_float == other[0, 0, 0], other[1, 0, 0], 0.0)
    return counts


def local(acts, token_ids, turn_ids, value_weight, norm_gain, query_grad):
    n_yhi, n_x = lax.axis_size("yhi"), lax.axis_size("x")
    inputs = acts.reshape(acts.shape[1], n_yhi, n_x, -1).transpose(0, 2, 1, 3)
    inputs = inputs.reshape(acts.shape[1], acts.shape[2])
    ids = turn_ids.reshape(-1)
    features = value_weight.shape[1]
    n_group = lax.axis_size(GROUP)
    turn_total = TURN_DEV * lax.axis_size(SHARD) * n_group
    cols = features // n_group
    me = lax.axis_index(GROUP)
    core = lax.axis_index("core")
    text_mask = (token_ids.reshape(-1) < first_special).astype(jnp.float32)

    def own(array):
        return lax.dynamic_slice(array, (0, me * cols), (array.shape[0], cols))

    def project(halves):
        return jnp.concatenate(
            [jnp.dot(inputs, half, preferred_element_type=jnp.float32) for half in halves], axis=1
        )

    gain = norm_gain.reshape(2, 2, cols)
    gain = jnp.concatenate(
        [jnp.where(core == 0, gain[:, 0], gain[:, 1]), jnp.where(core == 0, gain[:, 1], gain[:, 0])]
    ).reshape(-1)
    gain_square = gain * gain
    query = own(query_grad)

    both = gather_line(jnp.concatenate([own(value_weight), query.astype(jnp.bfloat16)], axis=1))
    values = project(gather_rows([piece[:, :cols] for piece in both]))
    tangent = project(gather_rows([piece[:, cols:] for piece in both]))
    own_count = turn_counts(text_mask, ids)
    turn_weight = text_mask / (jnp.maximum(own_count, 1.0) * jnp.float32(turn_total))
    root_mean = jnp.sqrt(jnp.mean(values * values, axis=-1, keepdims=True) + 1e-06)
    unit_values = values / root_mean
    estimate = query
    for step in range(ITERS):
        if step:
            tangent = project(gather_rows(gather_line(estimate.astype(jnp.bfloat16))))
        inner = gain_square * norm_jacobian(tangent, unit_values, root_mean)
        adjoint = (turn_weight[:, None] * norm_jacobian(inner, unit_values, root_mean)).astype(
            jnp.bfloat16
        )
        curvature = reduce_blocks(inputs, adjoint)
        estimate = query + estimate - (curvature + damping * estimate) / lissa_scale
    whole = spread(estimate, GROUP)
    return jnp.concatenate([whole[i] for i in range(n_group)], axis=1)


def solution(mesh):
    fine = Mesh(mesh.devices.reshape(2, 2, 2, 4, 8), FINE)
    placed = (
        P(GROUP, SHARD, None),
        P(GROUP, SHARD),
        P(GROUP, SHARD),
        P(SHARD, None),
        P(),
        P(SHARD, None),
    )
    return jax.shard_map(
        local, mesh=fine, in_specs=placed, out_specs=P(SHARD, None), check_vma=False
    )
```

```python
import jax
import jax.numpy as jnp
from jax import lax
from jax.experimental import pallas as pl
from jax.experimental.pallas import tpu as pltpu
from jax.sharding import Mesh, PartitionSpec as P

TURN_DEV = 4
ITERS = 2

damping = 1.0
lissa_scale = 12.0
first_special = 128000

FINE = ("ylo", "core", "yhi", "x", "z")
GROUP = ("ylo", "core")
SHARD = ("yhi", "x", "z")
PLANE = ("ylo", "yhi", "x")


def core_swap(value):
    return lax.ppermute(value, "core", [(0, 1), (1, 0)])


def exchange(blocks, axes):
    return lax.all_to_all(blocks, axes, split_axis=0, concat_axis=0, tiled=True)


def spread(block, axes):
    n = lax.axis_size(axes)
    return exchange(jnp.broadcast_to(block[None], (n,) + block.shape), axes)


def gather_plane(block):
    plane = spread(block, PLANE)
    n = lax.axis_size("ylo")
    mine = plane.reshape((n, plane.shape[0] // n) + block.shape)
    return mine, core_swap(mine)


def gather_line(block):
    line = spread(block, "z")
    return line.reshape(line.shape[0] * line.shape[1], line.shape[2])


def kernel_params():
    return pltpu.CompilerParams(
        dimension_semantics=("arbitrary",), vmem_limit_bytes=32 * 1024 * 1024
    )


def times_rows(acts_ref, rows_ref):
    rows = jnp.concatenate([rows_ref[0, 0], rows_ref[1, 0]], axis=1)
    return jnp.dot(acts_ref[...], rows, preferred_element_type=jnp.float32)


def project_kernel(acts_ref, rows_ref, out_ref):
    part = times_rows(acts_ref, rows_ref)

    @pl.when(pl.program_id(0) == 0)
    def _():
        out_ref[...] = part

    @pl.when(pl.program_id(0) > 0)
    def _():
        out_ref[...] += part


def project(inputs, rows):
    n_low, n_chunk, chunk, cols = rows.shape
    tokens = inputs.shape[0]
    return pl.pallas_call(
        project_kernel,
        grid=(n_chunk,),
        in_specs=[
            pl.BlockSpec((tokens, chunk), lambda i: (0, i)),
            pl.BlockSpec((n_low, 1, chunk, cols), lambda i: (0, i, 0, 0)),
        ],
        out_specs=pl.BlockSpec((tokens, n_low * cols), lambda i: (0, 0)),
        out_shape=jax.ShapeDtypeStruct((tokens, n_low * cols), jnp.float32),
        compiler_params=kernel_params(),
        cost_estimate=pl.CostEstimate(
            flops=2 * inputs.size * n_low * cols,
            bytes_accessed=2 * (inputs.size + rows.size) + 4 * tokens * n_low * cols,
            transcendentals=0,
        ),
    )(inputs, rows)


def adjoint_kernel(
    n_chunk,
    acts_ref,
    rows_ref,
    tangent_ref,
    values_ref,
    other_values_ref,
    gain_ref,
    weight_ref,
    own_ref,
    sent_ref,
    total_ref,
    other_ref,
):
    step = pl.program_id(0)
    tokens, half = tangent_ref.shape
    features = 2 * half

    @pl.when(step == 0)
    def _():
        total_ref[...] = times_rows(acts_ref, rows_ref)

    @pl.when((step > 0) & (step < n_chunk))
    def _():
        total_ref[...] += times_rows(acts_ref, rows_ref)

    @pl.when(step == n_chunk - 1)
    def _():
        size = min(128, tokens)

        def mean(first, second):
            whole = jnp.sum(first, axis=-1, keepdims=True) + jnp.sum(second, axis=-1, keepdims=True)
            return whole * (1.0 / features)

        for start in range(0, tokens, size):
            at = slice(start, start + size)
            value = (values_ref[at, :], other_values_ref[at, :])
            tangent = (tangent_ref[at, :], total_ref[at, :])
            inverse = 1.0 / jnp.sqrt(mean(value[0] * value[0], value[1] * value[1]) + 1e-06)
            unit = [v * inverse for v in value]

            def jacobian(vector):
                inner = mean(unit[0] * vector[0], unit[1] * vector[1])
                return [(v - u * inner) * inverse for v, u in zip(vector, unit)]

            scaled = [gain_ref[i : i + 1, :] * v for i, v in enumerate(jacobian(tangent))]
            weight = weight_ref[at, :]
            own, other = [weight * v for v in jacobian(scaled)]
            own_ref[:, at] = own.T.astype(jnp.bfloat16)
            other_ref[:, at] = other.T.astype(jnp.bfloat16)

    @pl.when(step >= n_chunk)
    def _():
        block = jnp.dot(other_ref[...], acts_ref[...], preferred_element_type=jnp.float32)
        block = block.astype(jnp.bfloat16)
        sent_ref[0, 0] = block[: half // 2]
        sent_ref[1, 0] = block[half // 2 :]


def adjoint_products(inputs, rows, tangent, values, gain_square, weight):
    n_low, n_chunk, chunk, cols = rows.shape
    tokens, half = tangent.shape

    def whole(*shape):
        return pl.BlockSpec(shape, lambda i: (0,) * len(shape))

    return pl.pallas_call(
        lambda *refs: adjoint_kernel(n_chunk, *refs),
        grid=(2 * n_chunk,),
        in_specs=[
            pl.BlockSpec((tokens, chunk), lambda i: (0, i % n_chunk)),
            pl.BlockSpec(
                (n_low, 1, chunk, cols), lambda i: (0, jnp.minimum(i, n_chunk - 1), 0, 0)
            ),
            whole(tokens, half),
            whole(tokens, half),
            whole(tokens, half),
            whole(2, half),
            whole(tokens, 1),
        ],
        out_specs=[
            whole(half, tokens),
            pl.BlockSpec(
                (n_low, 1, cols, chunk), lambda i: (0, jnp.maximum(i - n_chunk, 0), 0, 0)
            ),
        ],
        out_shape=[
            jax.ShapeDtypeStruct((half, tokens), jnp.bfloat16),
            jax.ShapeDtypeStruct((n_low, n_chunk, cols, chunk), jnp.bfloat16),
        ],
        scratch_shapes=[
            pltpu.VMEM((tokens, half), jnp.float32),
            pltpu.VMEM((half, tokens), jnp.bfloat16),
        ],
        compiler_params=kernel_params(),
    )(inputs, rows, tangent, values[0], values[1], gain_square, weight)


def curvature_kernel(acts_ref, adjoint_ref, other_ref, out_ref):
    block = jnp.dot(adjoint_ref[...], acts_ref[...], preferred_element_type=jnp.float32)
    half = block.shape[0] // 2
    for i in range(2):
        total = block[i * half : (i + 1) * half] + other_ref[i, 0].astype(jnp.float32)
        out_ref[i, 0] = total.astype(jnp.bfloat16)


def curvature_blocks(inputs, adjoint, other):
    n_low, n_chunk, cols, chunk = other.shape
    tokens = inputs.shape[0]
    piece = pl.BlockSpec((n_low, 1, cols, chunk), lambda i: (0, i, 0, 0))
    return pl.pallas_call(
        curvature_kernel,
        grid=(n_chunk,),
        in_specs=[
            pl.BlockSpec((tokens, chunk), lambda i: (0, i)),
            pl.BlockSpec(adjoint.shape, lambda i: (0, 0)),
            piece,
        ],
        out_specs=piece,
        out_shape=jax.ShapeDtypeStruct(other.shape, jnp.bfloat16),
        compiler_params=kernel_params(),
    )(inputs, adjoint, other)


def reduce_blocks(blocks):
    n_low, n_chunk, cols, chunk = blocks.shape
    n_line = lax.axis_size("z")
    parts = exchange(blocks.reshape(n_low * n_chunk, cols, chunk), PLANE)
    line = jnp.sum(parts.astype(jnp.float32), axis=0).astype(jnp.bfloat16)
    line = line.reshape(cols, n_line, chunk // n_line).transpose(1, 2, 0)
    return jnp.sum(exchange(line, "z").astype(jnp.float32), axis=0)


def turn_counts(text_mask, turn_ids):
    n = lax.axis_size(SHARD)
    first, last = turn_ids[0], turn_ids[-1]

    def edge(turn):
        count = jnp.sum(jnp.where(turn_ids == turn, text_mask, 0.0))
        row = jnp.stack([turn.astype(jnp.float32), count])
        return jnp.broadcast_to(row[:, None, None], (2, 8, 128))

    left = lax.ppermute(edge(last), SHARD, [(i, i + 1) for i in range(n - 1)])
    right = lax.ppermute(edge(first), SHARD, [(i + 1, i) for i in range(n - 1)])
    same = turn_ids[:, None] == turn_ids[None, :]
    counts = jnp.sum(jnp.where(same, text_mask[None, :], 0.0), axis=1)
    as_float = turn_ids.astype(jnp.float32)
    for other in (left, right):
        counts = counts + jnp.where(as_float == other[0, 0, 0], other[1, 0, 0], 0.0)
    return counts


def local(acts, token_ids, turn_ids, value_weight, norm_gain, query_grad):
    inputs = acts.reshape(acts.shape[1], acts.shape[2])
    ids = turn_ids.reshape(-1)
    features = value_weight.shape[1]
    n_group = lax.axis_size(GROUP)
    turn_total = TURN_DEV * lax.axis_size(SHARD) * n_group
    cols = features // n_group
    me = lax.axis_index(GROUP)
    core = lax.axis_index("core")
    text_mask = (token_ids.reshape(-1) < first_special).astype(jnp.float32)

    def own(array):
        return lax.dynamic_slice(array, (0, me * cols), (array.shape[0], cols))

    gain = norm_gain.reshape(2, 2, cols)
    gain = jnp.stack(
        [jnp.where(core == 0, gain[:, 0], gain[:, 1]), jnp.where(core == 0, gain[:, 1], gain[:, 0])]
    ).reshape(2, -1)
    gain_square = gain * gain
    query = own(query_grad)

    both = gather_line(jnp.concatenate([own(value_weight), query.astype(jnp.bfloat16)], axis=1))
    values = [project(inputs, half) for half in gather_plane(both[:, :cols])]
    mine, other = gather_plane(both[:, cols:])
    own_count = turn_counts(text_mask, ids)
    turn_weight = text_mask / (jnp.maximum(own_count, 1.0) * jnp.float32(turn_total))
    weight = turn_weight[:, None]
    estimate = query
    for step in range(ITERS):
        if step:
            mine, other = gather_plane(gather_line(estimate.astype(jnp.bfloat16)))
        tangent = project(inputs, mine)
        adjoint, sent = adjoint_products(inputs, other, tangent, values, gain_square, weight)
        curvature = reduce_blocks(curvature_blocks(inputs, adjoint, core_swap(sent)))
        estimate = query + estimate - (curvature + damping * estimate) / lissa_scale
    whole = spread(estimate, GROUP)
    return jnp.concatenate([whole[i] for i in range(n_group)], axis=1)


def solution(mesh):
    fine = Mesh(mesh.devices.reshape(2, 2, 2, 4, 8), FINE)
    placed = (
        P(GROUP, SHARD, None),
        P(GROUP, SHARD),
        P(GROUP, SHARD),
        P(SHARD, None),
        P(),
        P(SHARD, None),
    )
    return jax.shard_map(
        local, mesh=fine, in_specs=placed, out_specs=P(SHARD, None), check_vma=False
    )
```

```python
import jax
import jax.numpy as jnp
from jax import lax
from jax.sharding import Mesh, PartitionSpec as P

TURN_DEV = 4
ITERS = 2

damping = 1.0
lissa_scale = 12.0
first_special = 128000

FINE = ("ylo", "core", "yhi", "x", "z")
GROUP = ("ylo", "core")
SHARD = ("yhi", "x", "z")
PLANE = ("ylo", "yhi", "x")


def core_swap(value):
    return lax.ppermute(value, "core", [(0, 1), (1, 0)])


def exchange(blocks, axes):
    return lax.all_to_all(blocks, axes, split_axis=0, concat_axis=0, tiled=True)


def spread(block, axes):
    n = lax.axis_size(axes)
    return exchange(jnp.broadcast_to(block[None], (n,) + block.shape), axes)


def gather_plane(block):
    plane = spread(block, PLANE)
    n = lax.axis_size("ylo")
    plane = plane.reshape(n, plane.shape[0] // n * plane.shape[1], plane.shape[2])
    return [plane[i] for i in range(n)]


def gather_line(block):
    line = spread(block, "z")
    return line.reshape(line.shape[0] * line.shape[1], line.shape[2])


def reduce_blocks(inputs, adjoint):
    half = adjoint.shape[1] // 2

    def outer(part):
        return lax.dot_general(
            part, inputs, (((0,), (0,)), ((), ())), preferred_element_type=jnp.float32
        )

    other = core_swap(outer(adjoint[:, half:]).astype(jnp.bfloat16))
    chip = (outer(adjoint[:, :half]) + other.astype(jnp.float32)).astype(jnp.bfloat16)
    n_low, n_plane, n_line = lax.axis_size("ylo"), lax.axis_size(PLANE), lax.axis_size("z")
    cols = half // n_low
    blocks = chip.reshape(n_low, cols, n_plane // n_low, -1).transpose(0, 2, 1, 3)
    parts = exchange(blocks.reshape(n_plane, cols, -1), PLANE)
    line = jnp.sum(parts.astype(jnp.float32), axis=0).astype(jnp.bfloat16)
    line = line.reshape(cols, n_line, -1).transpose(1, 2, 0)
    return jnp.sum(exchange(line, "z").astype(jnp.float32), axis=0)


def norm_jacobian(vector, unit_values, root_mean):
    inner = jnp.mean(unit_values * vector, axis=-1, keepdims=True)
    return (vector - unit_values * inner) / root_mean


def turn_counts(text_mask, turn_ids):
    n = lax.axis_size(SHARD)
    first, last = turn_ids[0], turn_ids[-1]

    def edge(turn):
        count = jnp.sum(jnp.where(turn_ids == turn, text_mask, 0.0))
        row = jnp.stack([turn.astype(jnp.float32), count])
        return jnp.broadcast_to(row[:, None, None], (2, 8, 128))

    left = lax.ppermute(edge(last), SHARD, [(i, i + 1) for i in range(n - 1)])
    right = lax.ppermute(edge(first), SHARD, [(i + 1, i) for i in range(n - 1)])
    ids = jnp.concatenate([turn_ids.astype(jnp.float32), left[0, 0, :1], right[0, 0, :1]])
    texts = jnp.concatenate([text_mask, left[1, 0, :1], right[1, 0, :1]])
    same = turn_ids.astype(jnp.float32)[:, None] == ids[None, :]
    return jnp.sum(jnp.where(same, texts[None, :], 0.0), axis=1)


def local(acts, token_ids, turn_ids, value_weight, norm_gain, query_grad):
    inputs = acts.reshape(acts.shape[1], acts.shape[2])
    ids = turn_ids.reshape(-1)
    features = value_weight.shape[1]
    n_group = lax.axis_size(GROUP)
    turn_total = TURN_DEV * lax.axis_size(SHARD) * n_group
    cols = features // n_group
    me = lax.axis_index(GROUP)
    core = lax.axis_index("core")
    text_mask = (token_ids.reshape(-1) < first_special).astype(jnp.float32)

    def own(array):
        return lax.dynamic_slice(array, (0, me * cols), (array.shape[0], cols))

    def times(rows):
        return jnp.dot(inputs, rows, preferred_element_type=jnp.float32)

    gain = norm_gain.reshape(2, 2, cols)
    gain = jnp.concatenate(
        [jnp.where(core == 0, gain[:, 0], gain[:, 1]), jnp.where(core == 0, gain[:, 1], gain[:, 0])]
    ).reshape(-1)
    gain_square = gain * gain
    query = own(query_grad)

    own_count = turn_counts(text_mask, ids)
    turn_weight = text_mask / (jnp.maximum(own_count, 1.0) * jnp.float32(turn_total))
    both = gather_line(jnp.concatenate([own(value_weight), query.astype(jnp.bfloat16)], axis=1))
    both, turn_weight = lax.optimization_barrier((both, turn_weight))
    mine = gather_plane(both)
    products = [times(rows) for rows in mine + [core_swap(rows) for rows in mine]]
    values = jnp.concatenate([product[:, :cols] for product in products], axis=1)
    tangent = jnp.concatenate([product[:, cols:] for product in products], axis=1)
    root_mean = jnp.sqrt(jnp.mean(values * values, axis=-1, keepdims=True) + 1e-06)
    unit_values = values / root_mean
    estimate = query
    for step in range(ITERS):
        if step:
            mine = jnp.stack(gather_plane(gather_line(estimate.astype(jnp.bfloat16))))
            halves = [jnp.concatenate([pair[0], pair[1]], axis=1) for pair in (mine, core_swap(mine))]
            tangent = jnp.concatenate([times(half) for half in halves], axis=1)
        inner = gain_square * norm_jacobian(tangent, unit_values, root_mean)
        adjoint = (turn_weight[:, None] * norm_jacobian(inner, unit_values, root_mean)).astype(
            jnp.bfloat16
        )
        curvature = reduce_blocks(inputs, adjoint)
        estimate = query + estimate - (curvature + damping * estimate) / lissa_scale
    whole = spread(estimate, GROUP)
    return jnp.concatenate([whole[i] for i in range(n_group)], axis=1)


def solution(mesh):
    fine = Mesh(mesh.devices.reshape(2, 2, 2, 4, 8), FINE)
    placed = (
        P(GROUP, SHARD, None),
        P(GROUP, SHARD),
        P(GROUP, SHARD),
        P(SHARD, None),
        P(),
        P(SHARD, None),
    )
    return jax.shard_map(
        local, mesh=fine, in_specs=placed, out_specs=P(SHARD, None), check_vma=False
    )
```

```python
import jax
import jax.numpy as jnp
from jax import lax
from jax.sharding import Mesh, PartitionSpec as P

TURN_DEV = 4
ITERS = 2

damping = 1.0
lissa_scale = 12.0
first_special = 128000

FINE = ("ylo", "core", "yhi", "x", "z")
GROUP = ("ylo", "core")
SHARD = ("yhi", "x", "z")
PLANE = ("ylo", "yhi", "x")


def core_swap(value):
    return lax.ppermute(value, "core", [(0, 1), (1, 0)])


def exchange(blocks, axes):
    return lax.all_to_all(blocks, axes, split_axis=0, concat_axis=0, tiled=True)


def spread(block, axes):
    n = lax.axis_size(axes)
    return exchange(jnp.broadcast_to(block[None], (n,) + block.shape), axes)


def ring_gather(block):
    n = lax.axis_size("z")
    me = lax.axis_index("z")
    whole = jnp.zeros((block.shape[0], n) + block.shape[1:], block.dtype)

    def shift(value, step):
        return lax.ppermute(value, "z", [(i, (i + step) % n) for i in range(n)])

    def put(whole, piece, owner, start=0):
        return lax.dynamic_update_slice(whole, piece[:, None], (start, owner % n, 0, 0))

    whole = put(whole, block, me)
    before = after = block
    for step in range(1, n // 2):
        before, after = shift(before, 1), shift(after, -1)
        whole = put(whole, before, me + n - step)
        whole = put(whole, after, me + step)
    half = block.shape[0] // 2
    whole = put(whole, shift(before[:half], 1), me + n // 2)
    return put(whole, shift(after[half:], -1), me + n // 2, half)


def gather_ring(block):
    n = lax.axis_size("ylo")
    return ring_gather(spread(block, PLANE)).reshape(n, -1, block.shape[1])


def gather_plane(block):
    return spread(block, PLANE).reshape(lax.axis_size("ylo"), -1, block.shape[1])


def gather_line(block):
    line = spread(block, "z")
    return line.reshape(line.shape[0] * line.shape[1], line.shape[2])


def reduce_blocks(inputs, adjoint):
    half = adjoint.shape[1] // 2

    def outer(part):
        return lax.dot_general(
            part, inputs, (((0,), (0,)), ((), ())), preferred_element_type=jnp.float32
        )

    other = core_swap(outer(adjoint[:, half:]).astype(jnp.bfloat16))
    chip = (outer(adjoint[:, :half]) + other.astype(jnp.float32)).astype(jnp.bfloat16)
    n_low, n_plane, n_line = lax.axis_size("ylo"), lax.axis_size(PLANE), lax.axis_size("z")
    cols = half // n_low
    blocks = chip.reshape(n_low, cols, n_plane // n_low, -1).transpose(0, 2, 1, 3)
    parts = exchange(blocks.reshape(n_plane, cols, -1), PLANE)
    line = jnp.sum(parts.astype(jnp.float32), axis=0).astype(jnp.bfloat16)
    line = line.reshape(cols, n_line, -1).transpose(1, 2, 0)
    return jnp.sum(exchange(line, "z").astype(jnp.float32), axis=0)


def norm_jacobian(vector, unit_values, root_mean):
    inner = jnp.mean(unit_values * vector, axis=-1, keepdims=True)
    return (vector - unit_values * inner) / root_mean


def turn_counts(text_mask, turn_ids):
    n = lax.axis_size(SHARD)
    first, last = turn_ids[0], turn_ids[-1]

    def edge(turn):
        count = jnp.sum(jnp.where(turn_ids == turn, text_mask, 0.0))
        row = jnp.stack([turn.astype(jnp.float32), count])
        return jnp.broadcast_to(row[:, None, None], (2, 8, 128))

    left = lax.ppermute(edge(last), SHARD, [(i, i + 1) for i in range(n - 1)])
    right = lax.ppermute(edge(first), SHARD, [(i + 1, i) for i in range(n - 1)])
    ids = jnp.concatenate([turn_ids.astype(jnp.float32), left[0, 0, :1], right[0, 0, :1]])
    texts = jnp.concatenate([text_mask, left[1, 0, :1], right[1, 0, :1]])
    same = turn_ids.astype(jnp.float32)[:, None] == ids[None, :]
    return jnp.sum(jnp.where(same, texts[None, :], 0.0), axis=1)


def local(acts, token_ids, turn_ids, value_weight, norm_gain, query_grad):
    inputs = acts.reshape(acts.shape[1], acts.shape[2])
    ids = turn_ids.reshape(-1)
    features = value_weight.shape[1]
    n_group = lax.axis_size(GROUP)
    turn_total = TURN_DEV * lax.axis_size(SHARD) * n_group
    cols = features // n_group
    me = lax.axis_index(GROUP)
    core = lax.axis_index("core")
    text_mask = (token_ids.reshape(-1) < first_special).astype(jnp.float32)

    def own(array):
        return lax.dynamic_slice(array, (0, me * cols), (array.shape[0], cols))

    def project(mine):
        halves = [jnp.concatenate([pair[0], pair[1]], axis=1) for pair in (mine, core_swap(mine))]
        return jnp.concatenate(
            [jnp.dot(inputs, half, preferred_element_type=jnp.float32) for half in halves], axis=1
        )

    gain = norm_gain.reshape(2, 2, cols)
    gain = jnp.concatenate(
        [jnp.where(core == 0, gain[:, 0], gain[:, 1]), jnp.where(core == 0, gain[:, 1], gain[:, 0])]
    ).reshape(-1)
    gain_square = gain * gain
    query = own(query_grad)

    own_count = turn_counts(text_mask, ids)
    turn_weight = text_mask / (jnp.maximum(own_count, 1.0) * jnp.float32(turn_total))
    tangent = project(gather_ring(query.astype(jnp.bfloat16)))
    values = project(gather_plane(gather_line(own(value_weight))))
    root_mean = jnp.sqrt(jnp.mean(values * values, axis=-1, keepdims=True) + 1e-06)
    unit_values = values / root_mean
    estimate = query
    for step in range(ITERS):
        if step:
            tangent = project(gather_plane(gather_line(estimate.astype(jnp.bfloat16))))
        inner = gain_square * norm_jacobian(tangent, unit_values, root_mean)
        adjoint = (turn_weight[:, None] * norm_jacobian(inner, unit_values, root_mean)).astype(
            jnp.bfloat16
        )
        curvature = reduce_blocks(inputs, adjoint)
        estimate = query + estimate - (curvature + damping * estimate) / lissa_scale
    whole = spread(estimate, GROUP)
    return jnp.concatenate([whole[i] for i in range(n_group)], axis=1)


def solution(mesh):
    fine = Mesh(mesh.devices.reshape(2, 2, 2, 4, 8), FINE)
    placed = (
        P(GROUP, SHARD, None),
        P(GROUP, SHARD),
        P(GROUP, SHARD),
        P(SHARD, None),
        P(),
        P(SHARD, None),
    )
    return jax.shard_map(
        local, mesh=fine, in_specs=placed, out_specs=P(SHARD, None), check_vma=False
    )
```

```python
import jax
import jax.numpy as jnp
from jax import lax
from jax.sharding import Mesh, PartitionSpec as P

TURN_DEV = 4
ITERS = 2

damping = 1.0
lissa_scale = 12.0
first_special = 128000

FINE = ("ylo", "core", "yhi", "x", "z")
GROUP = ("ylo", "core")
SHARD = ("yhi", "x", "z")
PLANE = ("ylo", "yhi", "x")


def core_swap(value):
    return lax.ppermute(value, "core", [(0, 1), (1, 0)])


def exchange(blocks, axes):
    return lax.all_to_all(blocks, axes, split_axis=0, concat_axis=0, tiled=True)


def spread(block, axes):
    n = lax.axis_size(axes)
    return exchange(jnp.broadcast_to(block[None], (n,) + block.shape), axes)


def ring_gather(block):
    n = lax.axis_size("z")
    me = lax.axis_index("z")
    whole = jnp.zeros((block.shape[0], n) + block.shape[1:], block.dtype)

    def shift(value, step):
        return lax.ppermute(value, "z", [(i, (i + step) % n) for i in range(n)])

    def put(whole, piece, owner, start=0):
        return lax.dynamic_update_slice(whole, piece[:, None], (start, owner % n, 0, 0))

    whole = put(whole, block, me)
    before = after = block
    for step in range(1, n // 2):
        before, after = shift(before, 1), shift(after, -1)
        whole = put(whole, before, me + n - step)
        whole = put(whole, after, me + step)
    half = block.shape[0] // 2
    whole = put(whole, shift(before[:half], 1), me + n // 2)
    return put(whole, shift(after[half:], -1), me + n // 2, half)


def gather_plane(block):
    return spread(block, PLANE).reshape(lax.axis_size("ylo"), -1, block.shape[1])


def gather_line(block):
    line = spread(block, "z")
    return line.reshape(line.shape[0] * line.shape[1], line.shape[2])


def reduce_blocks(inputs, adjoint):
    half = adjoint.shape[1] // 2

    def outer(part):
        return lax.dot_general(
            part, inputs, (((0,), (0,)), ((), ())), preferred_element_type=jnp.float32
        )

    other = core_swap(outer(adjoint[:, half:]).astype(jnp.bfloat16))
    chip = (outer(adjoint[:, :half]) + other.astype(jnp.float32)).astype(jnp.bfloat16)
    n_low, n_plane, n_line = lax.axis_size("ylo"), lax.axis_size(PLANE), lax.axis_size("z")
    cols = half // n_low
    blocks = chip.reshape(n_low, cols, n_plane // n_low, -1).transpose(0, 2, 1, 3)
    parts = exchange(blocks.reshape(n_plane, cols, -1), PLANE)
    line = jnp.sum(parts.astype(jnp.float32), axis=0).astype(jnp.bfloat16)
    line = line.reshape(cols, n_line, -1).transpose(1, 2, 0)
    return jnp.sum(exchange(line, "z").astype(jnp.float32), axis=0)


def norm_jacobian(vector, unit_values, root_mean):
    inner = jnp.mean(unit_values * vector, axis=-1, keepdims=True)
    return (vector - unit_values * inner) / root_mean


def turn_counts(text_mask, turn_ids):
    n = lax.axis_size(SHARD)
    turns = turn_ids.astype(jnp.float32)
    here = jnp.stack([turns, text_mask])
    left = lax.ppermute(here, SHARD, [(i, i + 1) for i in range(n - 1)])
    right = lax.ppermute(here, SHARD, [(i + 1, i) for i in range(n - 1)])
    return sum(
        jnp.sum(jnp.where(turns[:, None] == other[0][None, :], other[1][None, :], 0.0), axis=1)
        for other in (here, left, right)
    )


def local(acts, token_ids, turn_ids, value_weight, norm_gain, query_grad):
    inputs = acts.reshape(acts.shape[1], acts.shape[2])
    ids = turn_ids.reshape(-1)
    features = value_weight.shape[1]
    n_group = lax.axis_size(GROUP)
    turn_total = TURN_DEV * lax.axis_size(SHARD) * n_group
    cols = features // n_group
    me = lax.axis_index(GROUP)
    core = lax.axis_index("core")
    text_mask = (token_ids.reshape(-1) < first_special).astype(jnp.float32)

    def own(array):
        return lax.dynamic_slice(array, (0, me * cols), (array.shape[0], cols))

    def project(mine):
        halves = [jnp.concatenate([pair[0], pair[1]], axis=1) for pair in (mine, core_swap(mine))]
        return jnp.concatenate(
            [jnp.dot(inputs, half, preferred_element_type=jnp.float32) for half in halves], axis=1
        )

    gain = norm_gain.reshape(2, 2, cols)
    gain = jnp.concatenate(
        [jnp.where(core == 0, gain[:, 0], gain[:, 1]), jnp.where(core == 0, gain[:, 1], gain[:, 0])]
    ).reshape(-1)
    gain_square = gain * gain
    query = own(query_grad)

    line = gather_line(own(value_weight))
    block, line = lax.optimization_barrier((query.astype(jnp.bfloat16), line))
    plane = spread(block, PLANE)
    plane, line = lax.optimization_barrier((plane, line))
    tangent = project(ring_gather(plane).reshape(lax.axis_size("ylo"), -1, cols))
    values = project(gather_plane(line))
    own_count = turn_counts(text_mask, ids)
    turn_weight = text_mask / (jnp.maximum(own_count, 1.0) * jnp.float32(turn_total))
    root_mean = jnp.sqrt(jnp.mean(values * values, axis=-1, keepdims=True) + 1e-06)
    unit_values = values / root_mean
    estimate = query
    for step in range(ITERS):
        if step:
            tangent = project(gather_plane(gather_line(estimate.astype(jnp.bfloat16))))
        inner = gain_square * norm_jacobian(tangent, unit_values, root_mean)
        adjoint = (turn_weight[:, None] * norm_jacobian(inner, unit_values, root_mean)).astype(
            jnp.bfloat16
        )
        curvature = reduce_blocks(inputs, adjoint)
        estimate = query + estimate - (curvature + damping * estimate) / lissa_scale
    whole = spread(estimate, GROUP)
    return jnp.concatenate([whole[i] for i in range(n_group)], axis=1)


def solution(mesh):
    fine = Mesh(mesh.devices.reshape(2, 2, 2, 4, 8), FINE)
    placed = (
        P(GROUP, SHARD, None),
        P(GROUP, SHARD),
        P(GROUP, SHARD),
        P(SHARD, None),
        P(),
        P(SHARD, None),
    )
    return jax.shard_map(
        local, mesh=fine, in_specs=placed, out_specs=P(SHARD, None), check_vma=False
    )
```

```python
import jax
import jax.numpy as jnp
from jax import lax
from jax.sharding import Mesh, PartitionSpec as P

TURN_DEV = 4
ITERS = 2

damping = 1.0
lissa_scale = 12.0
first_special = 128000

FINE = ("ylo", "core", "yhi", "x", "z")
GROUP = ("ylo", "core")
SHARD = ("yhi", "x", "z")
PLANE = ("ylo", "yhi", "x")


def core_swap(value):
    return lax.ppermute(value, "core", [(0, 1), (1, 0)])


def exchange(blocks, axes):
    return lax.all_to_all(blocks, axes, split_axis=0, concat_axis=0, tiled=True)


def spread(block, axes):
    n = lax.axis_size(axes)
    return exchange(jnp.broadcast_to(block[None], (n,) + block.shape), axes)


def ring_gather(block):
    n = lax.axis_size("z")
    me = lax.axis_index("z")
    wholes = [jnp.zeros((block.shape[1], n) + block.shape[2:], block.dtype) for _ in range(2)]

    def shift(value, step):
        return lax.ppermute(value, "z", [(i, (i + step) % n) for i in range(n)])

    def put(index, piece, owner):
        wholes[index] = lax.dynamic_update_slice(
            wholes[index], piece[:, None], (0, owner % n, 0, 0)
        )

    before = after = block
    for index in range(2):
        put(index, block[index], me)
    for step in range(1, n // 2):
        before, after = shift(before, 1), shift(after, -1)
        for index in range(2):
            put(index, before[index], me + n - step)
            put(index, after[index], me + step)
    put(0, shift(before[0], 1), me + n // 2)
    put(1, shift(after[1], -1), me + n // 2)
    return [whole.reshape(-1, block.shape[3]) for whole in wholes]


def double_line(block, bit):
    other = lax.ppermute(block, "z", [(i, i ^ bit) for i in range(lax.axis_size("z"))])
    low = (lax.axis_index("z") & bit) == 0
    return jnp.concatenate([jnp.where(low, block, other), jnp.where(low, other, block)], axis=0)


def gather_plane(block):
    return spread(block, PLANE).reshape(lax.axis_size("ylo"), -1, block.shape[1])


def gather_line(block):
    line = spread(block, "z")
    return line.reshape(line.shape[0] * line.shape[1], line.shape[2])


def reduce_blocks(inputs, adjoint):
    half = adjoint.shape[1] // 2

    def outer(part):
        return lax.dot_general(
            part, inputs, (((0,), (0,)), ((), ())), preferred_element_type=jnp.float32
        )

    other = core_swap(outer(adjoint[:, half:]).astype(jnp.bfloat16))
    chip = (outer(adjoint[:, :half]) + other.astype(jnp.float32)).astype(jnp.bfloat16)
    n_low, n_plane, n_line = lax.axis_size("ylo"), lax.axis_size(PLANE), lax.axis_size("z")
    cols = half // n_low
    blocks = chip.reshape(n_low, cols, n_plane // n_low, -1).transpose(0, 2, 1, 3)
    parts = exchange(blocks.reshape(n_plane, cols, -1), PLANE)
    line = jnp.sum(parts.astype(jnp.float32), axis=0).astype(jnp.bfloat16)
    line = line.reshape(cols, n_line, -1).transpose(1, 2, 0)
    return jnp.sum(exchange(line, "z").astype(jnp.float32), axis=0)


def norm_jacobian(vector, unit_values, root_mean):
    inner = jnp.mean(unit_values * vector, axis=-1, keepdims=True)
    return (vector - unit_values * inner) / root_mean


def turn_counts(text_mask, turn_ids):
    n = lax.axis_size(SHARD)
    turns = turn_ids.astype(jnp.float32)
    here = jnp.stack([turns, text_mask])
    left = lax.ppermute(here, SHARD, [(i, i + 1) for i in range(n - 1)])
    right = lax.ppermute(here, SHARD, [(i + 1, i) for i in range(n - 1)])
    return sum(
        jnp.sum(jnp.where(turns[:, None] == other[0][None, :], other[1][None, :], 0.0), axis=1)
        for other in (here, left, right)
    )


def local(acts, token_ids, turn_ids, value_weight, norm_gain, query_grad):
    inputs = acts.reshape(acts.shape[1], acts.shape[2])
    ids = turn_ids.reshape(-1)
    features = value_weight.shape[1]
    n_group = lax.axis_size(GROUP)
    turn_total = TURN_DEV * lax.axis_size(SHARD) * n_group
    cols = features // n_group
    me = lax.axis_index(GROUP)
    core = lax.axis_index("core")
    text_mask = (token_ids.reshape(-1) < first_special).astype(jnp.float32)

    def own(array):
        return lax.dynamic_slice(array, (0, me * cols), (array.shape[0], cols))

    def project(mine, others):
        halves = [jnp.concatenate(pair, axis=1) for pair in (mine, others)]
        return jnp.concatenate(
            [jnp.dot(inputs, half, preferred_element_type=jnp.float32) for half in halves], axis=1
        )

    def project_plane(block):
        mine = gather_plane(block)
        other = core_swap(mine)
        return project([mine[0], mine[1]], [other[0], other[1]])

    gain = norm_gain.reshape(2, 2, cols)
    gain = jnp.concatenate(
        [jnp.where(core == 0, gain[:, 0], gain[:, 1]), jnp.where(core == 0, gain[:, 1], gain[:, 0])]
    ).reshape(-1)
    gain_square = gain * gain
    query = own(query_grad)

    line = double_line(own(value_weight), 1)
    line, ids, text_mask = lax.optimization_barrier((line, ids, text_mask))
    line = double_line(double_line(line, 2), 4)
    plane = spread(query.astype(jnp.bfloat16), PLANE)
    plane, line = lax.optimization_barrier((plane, line))
    rows = ring_gather(plane.reshape((2, plane.shape[0] // 2) + plane.shape[1:]))
    tangent = project(rows, [core_swap(half) for half in rows])
    values = project_plane(line)
    own_count = turn_counts(text_mask, ids)
    turn_weight = text_mask / (jnp.maximum(own_count, 1.0) * jnp.float32(turn_total))
    root_mean = jnp.sqrt(jnp.mean(values * values, axis=-1, keepdims=True) + 1e-06)
    unit_values = values / root_mean
    estimate = query
    for step in range(ITERS):
        if step:
            tangent = project_plane(gather_line(estimate.astype(jnp.bfloat16)))
        inner = gain_square * norm_jacobian(tangent, unit_values, root_mean)
        adjoint = (turn_weight[:, None] * norm_jacobian(inner, unit_values, root_mean)).astype(
            jnp.bfloat16
        )
        curvature = reduce_blocks(inputs, adjoint)
        estimate = query + estimate - (curvature + damping * estimate) / lissa_scale
    whole = spread(estimate, GROUP)
    return jnp.concatenate([whole[i] for i in range(n_group)], axis=1)


def solution(mesh):
    fine = Mesh(mesh.devices.reshape(2, 2, 2, 4, 8), FINE)
    placed = (
        P(GROUP, SHARD, None),
        P(GROUP, SHARD),
        P(GROUP, SHARD),
        P(SHARD, None),
        P(),
        P(SHARD, None),
    )
    return jax.shard_map(
        local, mesh=fine, in_specs=placed, out_specs=P(SHARD, None), check_vma=False
    )
```

```python
import jax
import jax.numpy as jnp
from jax import lax
from jax.sharding import Mesh, PartitionSpec as P

TURN_DEV = 4
ITERS = 2

damping = 1.0
lissa_scale = 12.0
first_special = 128000

FINE = ("ylo", "core", "yhi", "x", "z")
GROUP = ("ylo", "core")
SHARD = ("yhi", "x", "z")
PLANE = ("ylo", "yhi", "x")


def core_swap(value):
    return lax.ppermute(value, "core", [(0, 1), (1, 0)])


def exchange(blocks, axes):
    return lax.all_to_all(blocks, axes, split_axis=0, concat_axis=0, tiled=True)


def spread(block, axes):
    n = lax.axis_size(axes)
    return exchange(jnp.broadcast_to(block[None], (n,) + block.shape), axes)


def ring_gather(block):
    n = lax.axis_size("z")
    me = lax.axis_index("z")
    wholes = [jnp.zeros((block.shape[1], n) + block.shape[2:], block.dtype) for _ in range(2)]

    def shift(value, step):
        return lax.ppermute(value, "z", [(i, (i + step) % n) for i in range(n)])

    def put(index, piece, owner):
        wholes[index] = lax.dynamic_update_slice(
            wholes[index], piece[:, None], (0, owner % n, 0, 0)
        )

    before = after = block
    for index in range(2):
        put(index, block[index], me)
    for step in range(1, n // 2):
        before, after = shift(before, 1), shift(after, -1)
        for index in range(2):
            put(index, before[index], me + n - step)
            put(index, after[index], me + step)
    put(0, shift(before[0], 1), me + n // 2)
    put(1, shift(after[1], -1), me + n // 2)
    return [whole.reshape(-1, block.shape[3]) for whole in wholes]


def gather_plane(block):
    return spread(block, PLANE).reshape(lax.axis_size("ylo"), -1, block.shape[1])


def gather_line(block):
    line = spread(block, "z")
    return line.reshape(line.shape[0] * line.shape[1], line.shape[2])


def reduce_blocks(inputs, adjoint):
    half = adjoint.shape[1] // 2

    def outer(part):
        return lax.dot_general(
            part, inputs, (((0,), (0,)), ((), ())), preferred_element_type=jnp.float32
        )

    other = core_swap(outer(adjoint[:, half:]).astype(jnp.bfloat16))
    chip = (outer(adjoint[:, :half]) + other.astype(jnp.float32)).astype(jnp.bfloat16)
    n_low, n_plane, n_line = lax.axis_size("ylo"), lax.axis_size(PLANE), lax.axis_size("z")
    cols = half // n_low
    blocks = chip.reshape(n_low, cols, n_plane // n_low, -1).transpose(0, 2, 1, 3)
    parts = exchange(blocks.reshape(n_plane, cols, -1), PLANE)
    line = jnp.sum(parts.astype(jnp.float32), axis=0).astype(jnp.bfloat16)
    line = line.reshape(cols, n_line, -1).transpose(1, 2, 0)
    return jnp.sum(exchange(line, "z").astype(jnp.float32), axis=0)


def norm_jacobian(vector, unit_values, root_mean):
    inner = jnp.mean(unit_values * vector, axis=-1, keepdims=True)
    return (vector - unit_values * inner) / root_mean


def turn_counts(text_mask, turn_ids):
    n = lax.axis_size(SHARD)
    turns = turn_ids.astype(jnp.float32)
    here = jnp.stack([turns, text_mask])
    left = lax.ppermute(here, SHARD, [(i, i + 1) for i in range(n - 1)])
    right = lax.ppermute(here, SHARD, [(i + 1, i) for i in range(n - 1)])
    return sum(
        jnp.sum(jnp.where(turns[:, None] == other[0][None, :], other[1][None, :], 0.0), axis=1)
        for other in (here, left, right)
    )


def local(acts, token_ids, turn_ids, value_weight, norm_gain, query_grad):
    inputs = acts.reshape(acts.shape[1], acts.shape[2])
    ids = turn_ids.reshape(-1)
    features = value_weight.shape[1]
    n_group = lax.axis_size(GROUP)
    turn_total = TURN_DEV * lax.axis_size(SHARD) * n_group
    cols = features // n_group
    me = lax.axis_index(GROUP)
    core = lax.axis_index("core")
    text_mask = (token_ids.reshape(-1) < first_special).astype(jnp.float32)

    def own(array):
        return lax.dynamic_slice(array, (0, me * cols), (array.shape[0], cols))

    def project(mine, others):
        halves = [jnp.concatenate(pair, axis=1) for pair in (mine, others)]
        return jnp.concatenate(
            [jnp.dot(inputs, half, preferred_element_type=jnp.float32) for half in halves], axis=1
        )

    def project_plane(block):
        mine = gather_plane(block)
        other = core_swap(mine)
        return project([mine[0], mine[1]], [other[0], other[1]])

    gain = norm_gain.reshape(2, 2, cols)
    gain = jnp.concatenate(
        [jnp.where(core == 0, gain[:, 0], gain[:, 1]), jnp.where(core == 0, gain[:, 1], gain[:, 0])]
    ).reshape(-1)
    gain_square = gain * gain
    query = own(query_grad)

    line = gather_line(own(value_weight))
    block, line = lax.optimization_barrier((query.astype(jnp.bfloat16), line))
    plane = spread(block, PLANE)
    plane, line = lax.optimization_barrier((plane, line))
    rows = ring_gather(plane.reshape((2, plane.shape[0] // 2) + plane.shape[1:]))
    tangent = project(rows, [core_swap(half) for half in rows])
    values = project_plane(line)
    own_count = turn_counts(text_mask, ids)
    turn_weight = text_mask / (jnp.maximum(own_count, 1.0) * jnp.float32(turn_total))
    root_mean = jnp.sqrt(jnp.mean(values * values, axis=-1, keepdims=True) + 1e-06)
    unit_values = values / root_mean
    estimate = query
    for step in range(ITERS):
        if step:
            tangent = project_plane(gather_line(estimate.astype(jnp.bfloat16)))
        inner = gain_square * norm_jacobian(tangent, unit_values, root_mean)
        adjoint = (turn_weight[:, None] * norm_jacobian(inner, unit_values, root_mean)).astype(
            jnp.bfloat16
        )
        curvature = reduce_blocks(inputs, adjoint)
        estimate = query + estimate - (curvature + damping * estimate) / lissa_scale
    whole = spread(estimate, GROUP)
    return jnp.concatenate([whole[i] for i in range(n_group)], axis=1)


def solution(mesh):
    fine = Mesh(mesh.devices.reshape(2, 2, 2, 4, 8), FINE)
    placed = (
        P(GROUP, SHARD, None),
        P(GROUP, SHARD),
        P(GROUP, SHARD),
        P(SHARD, None),
        P(),
        P(SHARD, None),
    )
    return jax.shard_map(
        local, mesh=fine, in_specs=placed, out_specs=P(SHARD, None), check_vma=False
    )
```

```python
import jax
import jax.numpy as jnp
from jax import lax
from jax.sharding import Mesh, PartitionSpec as P

TURN_DEV = 4
ITERS = 2

damping = 1.0
lissa_scale = 12.0
first_special = 128000

FINE = ("ylo", "core", "yhi", "x", "z")
GROUP = ("ylo", "core")
SHARD = ("yhi", "x", "z")
PLANE = ("ylo", "yhi", "x")


def core_swap(value):
    return lax.ppermute(value, "core", [(0, 1), (1, 0)])


def exchange(blocks, axes):
    return lax.all_to_all(blocks, axes, split_axis=0, concat_axis=0, tiled=True)


def spread(block, axes):
    n = lax.axis_size(axes)
    return exchange(jnp.broadcast_to(block[None], (n,) + block.shape), axes)


def ring_gather(block, later):
    n = lax.axis_size("z")
    me = lax.axis_index("z")
    wholes = [jnp.zeros((block.shape[1], n) + block.shape[2:], block.dtype) for _ in range(2)]

    def shift(value, step):
        return lax.ppermute(value, "z", [(i, (i + step) % n) for i in range(n)])

    def put(index, piece, owner):
        wholes[index] = lax.dynamic_update_slice(
            wholes[index], piece[:, None], (0, owner % n, 0, 0)
        )

    before = after = block
    for index in range(2):
        put(index, block[index], me)
    for step in range(1, n // 2):
        before, after = shift(before, 1), shift(after, -1)
        if step == 1:
            before, *later = lax.optimization_barrier((before, *later))
        for index in range(2):
            put(index, before[index], me + n - step)
            put(index, after[index], me + step)
    put(0, shift(before[0], 1), me + n // 2)
    put(1, shift(after[1], -1), me + n // 2)
    return [whole.reshape(-1, block.shape[3]) for whole in wholes], later


def gather_plane(block):
    return spread(block, PLANE).reshape(lax.axis_size("ylo"), -1, block.shape[1])


def gather_line(block):
    line = spread(block, "z")
    return line.reshape(line.shape[0] * line.shape[1], line.shape[2])


def reduce_blocks(inputs, adjoint):
    half = adjoint.shape[1] // 2

    def outer(part):
        return lax.dot_general(
            part, inputs, (((0,), (0,)), ((), ())), preferred_element_type=jnp.float32
        )

    other = core_swap(outer(adjoint[:, half:]).astype(jnp.bfloat16))
    chip = (outer(adjoint[:, :half]) + other.astype(jnp.float32)).astype(jnp.bfloat16)
    n_low, n_plane, n_line = lax.axis_size("ylo"), lax.axis_size(PLANE), lax.axis_size("z")
    cols = half // n_low
    blocks = chip.reshape(n_low, cols, n_plane // n_low, -1).transpose(0, 2, 1, 3)
    parts = exchange(blocks.reshape(n_plane, cols, -1), PLANE)
    line = jnp.sum(parts.astype(jnp.float32), axis=0).astype(jnp.bfloat16)
    line = line.reshape(cols, n_line, -1).transpose(1, 2, 0)
    return jnp.sum(exchange(line, "z").astype(jnp.float32), axis=0)


def norm_jacobian(vector, unit_values, root_mean):
    inner = jnp.mean(unit_values * vector, axis=-1, keepdims=True)
    return (vector - unit_values * inner) / root_mean


def turn_counts(text_mask, turn_ids):
    n = lax.axis_size(SHARD)
    turns = turn_ids.astype(jnp.float32)
    here = jnp.stack([turns, text_mask])
    left = lax.ppermute(here, SHARD, [(i, i + 1) for i in range(n - 1)])
    right = lax.ppermute(here, SHARD, [(i + 1, i) for i in range(n - 1)])
    return sum(
        jnp.sum(jnp.where(turns[:, None] == other[0][None, :], other[1][None, :], 0.0), axis=1)
        for other in (here, left, right)
    )


def local(acts, token_ids, turn_ids, value_weight, norm_gain, query_grad):
    inputs = acts.reshape(acts.shape[1], acts.shape[2])
    ids = turn_ids.reshape(-1)
    features = value_weight.shape[1]
    n_group = lax.axis_size(GROUP)
    turn_total = TURN_DEV * lax.axis_size(SHARD) * n_group
    cols = features // n_group
    me = lax.axis_index(GROUP)
    core = lax.axis_index("core")
    text_mask = (token_ids.reshape(-1) < first_special).astype(jnp.float32)

    def own(array):
        return lax.dynamic_slice(array, (0, me * cols), (array.shape[0], cols))

    def project(mine, others):
        halves = [jnp.concatenate(pair, axis=1) for pair in (mine, others)]
        return jnp.concatenate(
            [jnp.dot(inputs, half, preferred_element_type=jnp.float32) for half in halves], axis=1
        )

    def project_plane(block):
        mine = gather_plane(block)
        other = core_swap(mine)
        return project([mine[0], mine[1]], [other[0], other[1]])

    gain = norm_gain.reshape(2, 2, cols)
    gain = jnp.concatenate(
        [jnp.where(core == 0, gain[:, 0], gain[:, 1]), jnp.where(core == 0, gain[:, 1], gain[:, 0])]
    ).reshape(-1)
    gain_square = gain * gain
    query = own(query_grad)

    line = gather_line(own(value_weight))
    block, line = lax.optimization_barrier((query.astype(jnp.bfloat16), line))
    plane = spread(block, PLANE)
    plane, line = lax.optimization_barrier((plane, line))
    blocks = plane.reshape((2, plane.shape[0] // 2) + plane.shape[1:])
    rows, (ids, text_mask) = ring_gather(blocks, (ids, text_mask))
    tangent = project(rows, [core_swap(half) for half in rows])
    values = project_plane(line)
    own_count = turn_counts(text_mask, ids)
    turn_weight = text_mask / (jnp.maximum(own_count, 1.0) * jnp.float32(turn_total))
    root_mean = jnp.sqrt(jnp.mean(values * values, axis=-1, keepdims=True) + 1e-06)
    unit_values = values / root_mean
    estimate = query
    for step in range(ITERS):
        if step:
            tangent = project_plane(gather_line(estimate.astype(jnp.bfloat16)))
        inner = gain_square * norm_jacobian(tangent, unit_values, root_mean)
        adjoint = (turn_weight[:, None] * norm_jacobian(inner, unit_values, root_mean)).astype(
            jnp.bfloat16
        )
        curvature = reduce_blocks(inputs, adjoint)
        estimate = query + estimate - (curvature + damping * estimate) / lissa_scale
    whole = spread(estimate, GROUP)
    return jnp.concatenate([whole[i] for i in range(n_group)], axis=1)


def solution(mesh):
    fine = Mesh(mesh.devices.reshape(2, 2, 2, 4, 8), FINE)
    placed = (
        P(GROUP, SHARD, None),
        P(GROUP, SHARD),
        P(GROUP, SHARD),
        P(SHARD, None),
        P(),
        P(SHARD, None),
    )
    return jax.shard_map(
        local, mesh=fine, in_specs=placed, out_specs=P(SHARD, None), check_vma=False
    )
```

```python
import jax
import jax.numpy as jnp
from jax import lax
from jax.sharding import Mesh, PartitionSpec as P

TURN_DEV = 4
ITERS = 2

damping = 1.0
lissa_scale = 12.0
first_special = 128000

FINE = ("ylo", "core", "yhi", "x", "z")
GROUP = ("ylo", "core")
SHARD = ("yhi", "x", "z")
PLANE = ("ylo", "yhi", "x")


def core_swap(value):
    return lax.ppermute(value, "core", [(0, 1), (1, 0)])


def exchange(blocks, axes):
    return lax.all_to_all(blocks, axes, split_axis=0, concat_axis=0, tiled=True)


def spread(block, axes):
    n = lax.axis_size(axes)
    return exchange(jnp.broadcast_to(block[None], (n,) + block.shape), axes)


def ring_gather(block):
    n = lax.axis_size("z")
    me = lax.axis_index("z")
    whole = jnp.zeros((block.shape[0], n) + block.shape[1:], block.dtype)

    def shift(value, step):
        return lax.ppermute(value, "z", [(i, (i + step) % n) for i in range(n)])

    def put(whole, piece, owner, start=0):
        return lax.dynamic_update_slice(whole, piece[:, None], (start, owner % n, 0, 0))

    whole = put(whole, block, me)
    before = after = block
    for step in range(1, n // 2):
        before, after = shift(before, 1), shift(after, -1)
        whole = put(whole, before, me + n - step)
        whole = put(whole, after, me + step)
    half = block.shape[0] // 2
    whole = put(whole, shift(before[:half], 1), me + n // 2)
    return put(whole, shift(after[half:], -1), me + n // 2, half)


def gather_plane(block):
    return spread(block, PLANE).reshape(lax.axis_size("ylo"), -1, block.shape[1])


def gather_line(block):
    line = spread(block, "z")
    return line.reshape(line.shape[0] * line.shape[1], line.shape[2])


def reduce_blocks(inputs, other_inputs, adjoint):
    half = adjoint.shape[1] // 2

    def outer(part, rows):
        return lax.dot_general(
            part, rows, (((0,), (0,)), ((), ())), preferred_element_type=jnp.float32
        )

    swapped = core_swap(adjoint[:, half:])
    chip = outer(adjoint[:, :half], inputs) + outer(swapped, other_inputs)
    chip = chip.astype(jnp.bfloat16)
    n_low, n_plane, n_line = lax.axis_size("ylo"), lax.axis_size(PLANE), lax.axis_size("z")
    cols = half // n_low
    blocks = chip.reshape(n_low, cols, n_plane // n_low, -1).transpose(0, 2, 1, 3)
    parts = exchange(blocks.reshape(n_plane, cols, -1), PLANE)
    line = jnp.sum(parts.astype(jnp.float32), axis=0).astype(jnp.bfloat16)
    line = line.reshape(cols, n_line, -1).transpose(1, 2, 0)
    return jnp.sum(exchange(line, "z").astype(jnp.float32), axis=0)


def norm_jacobian(vector, unit_values, root_mean):
    inner = jnp.mean(unit_values * vector, axis=-1, keepdims=True)
    return (vector - unit_values * inner) / root_mean


def turn_counts(text_mask, turn_ids):
    n = lax.axis_size(SHARD)
    turns = turn_ids.astype(jnp.float32)
    here = jnp.stack([turns, text_mask])
    left = lax.ppermute(here, SHARD, [(i, i + 1) for i in range(n - 1)])
    right = lax.ppermute(here, SHARD, [(i + 1, i) for i in range(n - 1)])
    return sum(
        jnp.sum(jnp.where(turns[:, None] == other[0][None, :], other[1][None, :], 0.0), axis=1)
        for other in (here, left, right)
    )


def local(acts, token_ids, turn_ids, value_weight, norm_gain, query_grad):
    inputs = acts.reshape(acts.shape[1], acts.shape[2])
    ids = turn_ids.reshape(-1)
    features = value_weight.shape[1]
    n_group = lax.axis_size(GROUP)
    turn_total = TURN_DEV * lax.axis_size(SHARD) * n_group
    cols = features // n_group
    me = lax.axis_index(GROUP)
    core = lax.axis_index("core")
    text_mask = (token_ids.reshape(-1) < first_special).astype(jnp.float32)

    def own(array):
        return lax.dynamic_slice(array, (0, me * cols), (array.shape[0], cols))

    other_inputs = core_swap(inputs)

    def project(mine):
        half = jnp.concatenate([mine[0], mine[1]], axis=1)
        swapped = core_swap(jnp.dot(other_inputs, half, preferred_element_type=jnp.float32))
        own_part = jnp.dot(inputs, half, preferred_element_type=jnp.float32)
        return jnp.concatenate([own_part, swapped], axis=1)

    gain = norm_gain.reshape(2, 2, cols)
    gain = jnp.concatenate(
        [jnp.where(core == 0, gain[:, 0], gain[:, 1]), jnp.where(core == 0, gain[:, 1], gain[:, 0])]
    ).reshape(-1)
    gain_square = gain * gain
    query = own(query_grad)

    line = gather_line(own(value_weight))
    block, line = lax.optimization_barrier((query.astype(jnp.bfloat16), line))
    plane = spread(block, PLANE)
    plane, line = lax.optimization_barrier((plane, line))
    tangent = project(ring_gather(plane).reshape(lax.axis_size("ylo"), -1, cols))
    values = project(gather_plane(line))
    own_count = turn_counts(text_mask, ids)
    turn_weight = text_mask / (jnp.maximum(own_count, 1.0) * jnp.float32(turn_total))
    root_mean = jnp.sqrt(jnp.mean(values * values, axis=-1, keepdims=True) + 1e-06)
    unit_values = values / root_mean
    estimate = query
    for step in range(ITERS):
        if step:
            tangent = project(gather_plane(gather_line(estimate.astype(jnp.bfloat16))))
        inner = gain_square * norm_jacobian(tangent, unit_values, root_mean)
        adjoint = (turn_weight[:, None] * norm_jacobian(inner, unit_values, root_mean)).astype(
            jnp.bfloat16
        )
        curvature = reduce_blocks(inputs, other_inputs, adjoint)
        estimate = query + estimate - (curvature + damping * estimate) / lissa_scale
    whole = spread(estimate, GROUP)
    return jnp.concatenate([whole[i] for i in range(n_group)], axis=1)


def solution(mesh):
    fine = Mesh(mesh.devices.reshape(2, 2, 2, 4, 8), FINE)
    placed = (
        P(GROUP, SHARD, None),
        P(GROUP, SHARD),
        P(GROUP, SHARD),
        P(SHARD, None),
        P(),
        P(SHARD, None),
    )
    return jax.shard_map(
        local, mesh=fine, in_specs=placed, out_specs=P(SHARD, None), check_vma=False
    )
```

```python
import jax
import jax.numpy as jnp
from jax import lax
from jax.sharding import Mesh, PartitionSpec as P

TURN_DEV = 4
ITERS = 2

damping = 1.0
lissa_scale = 12.0
first_special = 128000

FINE = ("ylo", "core", "yhi", "x", "z")
GROUP = ("ylo", "core")
SHARD = ("yhi", "x", "z")
PLANE = ("ylo", "yhi", "x")


def core_swap(value):
    return lax.ppermute(value, "core", [(0, 1), (1, 0)])


def exchange(blocks, axes):
    return lax.all_to_all(blocks, axes, split_axis=0, concat_axis=0, tiled=True)


def spread(block, axes):
    n = lax.axis_size(axes)
    return exchange(jnp.broadcast_to(block[None], (n,) + block.shape), axes)


def ring_gather(block):
    n = lax.axis_size("z")
    me = lax.axis_index("z")
    whole = jnp.zeros((block.shape[0], n) + block.shape[1:], block.dtype)

    def shift(value, step):
        return lax.ppermute(value, "z", [(i, (i + step) % n) for i in range(n)])

    def put(whole, piece, owner, start=0):
        return lax.dynamic_update_slice(whole, piece[:, None], (start, owner % n, 0, 0))

    whole = put(whole, block, me)
    before = after = block
    for step in range(1, n // 2):
        before, after = shift(before, 1), shift(after, -1)
        whole = put(whole, before, me + n - step)
        whole = put(whole, after, me + step)
    half = block.shape[0] // 2
    whole = put(whole, shift(before[:half], 1), me + n // 2)
    return put(whole, shift(after[half:], -1), me + n // 2, half)


def gather_plane(block):
    return spread(block, PLANE).reshape(lax.axis_size("ylo"), -1, block.shape[1])


def gather_line(block):
    line = spread(block, "z")
    return line.reshape(line.shape[0] * line.shape[1], line.shape[2])


def reduce_blocks(inputs, other_inputs, adjoint):
    half = adjoint.shape[1] // 2

    def outer(part, rows):
        return lax.dot_general(
            part, rows, (((0,), (0,)), ((), ())), preferred_element_type=jnp.float32
        )

    swapped = core_swap(adjoint[:, half:])
    chip = outer(adjoint[:, :half], inputs) + outer(swapped, other_inputs)
    chip = chip.astype(jnp.bfloat16)
    n_low, n_plane, n_line = lax.axis_size("ylo"), lax.axis_size(PLANE), lax.axis_size("z")
    cols = half // n_low
    blocks = chip.reshape(n_low, cols, n_plane // n_low, -1).transpose(0, 2, 1, 3)
    parts = exchange(blocks.reshape(n_plane, cols, -1), PLANE)
    line = jnp.sum(parts.astype(jnp.float32), axis=0).astype(jnp.bfloat16)
    line = line.reshape(cols, n_line, -1).transpose(1, 2, 0)
    return jnp.sum(exchange(line, "z").astype(jnp.float32), axis=0)


def norm_jacobian(vector, unit_values, root_mean):
    inner = jnp.mean(unit_values * vector, axis=-1, keepdims=True)
    return (vector - unit_values * inner) / root_mean


def turn_rows(text_mask, turn_ids, cols):
    flat = jnp.concatenate([turn_ids.astype(jnp.float32), text_mask]).astype(jnp.bfloat16)
    return jnp.pad(flat, (0, -flat.shape[0] % (16 * cols))).reshape(-1, cols)


def turn_counts(text_mask, turn_ids, before, after):
    n = turn_ids.shape[0]
    turns = turn_ids.astype(jnp.float32)
    counts = jnp.sum(jnp.where(turns[:, None] == turns[None, :], text_mask[None, :], 0.0), axis=1)
    for rows, there in (before, after):
        flat = rows.astype(jnp.float32).reshape(-1)
        same = (turns[:, None] == flat[None, :n]) & there
        counts = counts + jnp.sum(jnp.where(same, flat[None, n : 2 * n], 0.0), axis=1)
    return counts


def local(acts, token_ids, turn_ids, value_weight, norm_gain, query_grad):
    inputs = acts.reshape(acts.shape[1], acts.shape[2])
    ids = turn_ids.reshape(-1)
    features = value_weight.shape[1]
    n_group = lax.axis_size(GROUP)
    turn_total = TURN_DEV * lax.axis_size(SHARD) * n_group
    cols = features // n_group
    me = lax.axis_index(GROUP)
    core = lax.axis_index("core")
    text_mask = (token_ids.reshape(-1) < first_special).astype(jnp.float32)

    def own(array):
        return lax.dynamic_slice(array, (0, me * cols), (array.shape[0], cols))

    other_inputs = core_swap(inputs)

    def project(mine):
        half = jnp.concatenate([mine[0], mine[1]], axis=1)
        swapped = core_swap(jnp.dot(other_inputs, half, preferred_element_type=jnp.float32))
        own_part = jnp.dot(inputs, half, preferred_element_type=jnp.float32)
        return jnp.concatenate([own_part, swapped], axis=1)

    gain = norm_gain.reshape(2, 2, cols)
    gain = jnp.concatenate(
        [jnp.where(core == 0, gain[:, 0], gain[:, 1]), jnp.where(core == 0, gain[:, 1], gain[:, 0])]
    ).reshape(-1)
    gain_square = gain * gain
    query = own(query_grad)

    n_z = lax.axis_size("z")
    tokens = turn_rows(text_mask, ids, cols)
    count = tokens.shape[0]
    rows = value_weight.shape[0]
    line = spread(jnp.concatenate([own(value_weight), tokens]), "z")
    line, tokens = line[:, :rows].reshape(-1, cols), line[:, rows:]
    block = jnp.concatenate([query.astype(jnp.bfloat16), tokens[0], tokens[n_z - 1]])
    block, line = lax.optimization_barrier((block, line))
    plane = spread(block, PLANE)
    plane, line = lax.optimization_barrier((plane, line))
    plane, ends = plane[:, :rows], plane[:, rows:]
    place, chain = lax.axis_index("z"), lax.axis_index(("yhi", "x"))
    n_chain = lax.axis_size(("yhi", "x"))
    base = lax.axis_index("ylo") * n_chain

    def pick(array, index):
        return lax.dynamic_index_in_dim(array, index, keepdims=False)

    before = jnp.where(
        place > 0,
        pick(tokens, jnp.maximum(place - 1, 0)),
        pick(ends, base + jnp.maximum(chain - 1, 0))[count:],
    )
    after = jnp.where(
        place < n_z - 1,
        pick(tokens, jnp.minimum(place + 1, n_z - 1)),
        pick(ends, base + jnp.minimum(chain + 1, n_chain - 1))[:count],
    )
    before = (before, (place > 0) | (chain > 0))
    after = (after, (place < n_z - 1) | (chain < n_chain - 1))
    tangent = project(ring_gather(plane).reshape(lax.axis_size("ylo"), -1, cols))
    values = project(gather_plane(line))
    own_count = turn_counts(text_mask, ids, before, after)
    turn_weight = text_mask / (jnp.maximum(own_count, 1.0) * jnp.float32(turn_total))
    root_mean = jnp.sqrt(jnp.mean(values * values, axis=-1, keepdims=True) + 1e-06)
    unit_values = values / root_mean
    estimate = query
    for step in range(ITERS):
        if step:
            tangent = project(gather_plane(gather_line(estimate.astype(jnp.bfloat16))))
        inner = gain_square * norm_jacobian(tangent, unit_values, root_mean)
        adjoint = (turn_weight[:, None] * norm_jacobian(inner, unit_values, root_mean)).astype(
            jnp.bfloat16
        )
        curvature = reduce_blocks(inputs, other_inputs, adjoint)
        estimate = query + estimate - (curvature + damping * estimate) / lissa_scale
    whole = spread(estimate, GROUP)
    return jnp.concatenate([whole[i] for i in range(n_group)], axis=1)


def solution(mesh):
    fine = Mesh(mesh.devices.reshape(2, 2, 2, 4, 8), FINE)
    placed = (
        P(GROUP, SHARD, None),
        P(GROUP, SHARD),
        P(GROUP, SHARD),
        P(SHARD, None),
        P(),
        P(SHARD, None),
    )
    return jax.shard_map(
        local, mesh=fine, in_specs=placed, out_specs=P(SHARD, None), check_vma=False
    )
```

```python
import jax
import jax.numpy as jnp
from jax import lax
from jax.sharding import Mesh, PartitionSpec as P

TURN_DEV = 4
ITERS = 2

damping = 1.0
lissa_scale = 12.0
first_special = 128000

FINE = ("ylo", "core", "yhi", "x", "z")
GROUP = ("ylo", "core")
SHARD = ("yhi", "x", "z")
PLANE = ("ylo", "yhi", "x")


def core_swap(value):
    return lax.ppermute(value, "core", [(0, 1), (1, 0)])


def exchange(blocks, axes):
    return lax.all_to_all(blocks, axes, split_axis=0, concat_axis=0, tiled=True)


def spread(block, axes):
    n = lax.axis_size(axes)
    return exchange(jnp.broadcast_to(block[None], (n,) + block.shape), axes)


def ring_gather(block):
    n = lax.axis_size("z")
    me = lax.axis_index("z")
    whole = jnp.zeros((block.shape[0], n) + block.shape[1:], block.dtype)

    def shift(value, step):
        return lax.ppermute(value, "z", [(i, (i + step) % n) for i in range(n)])

    def put(whole, piece, owner, start=0):
        return lax.dynamic_update_slice(whole, piece[:, None], (start, owner % n, 0, 0))

    whole = put(whole, block, me)
    before = after = block
    for step in range(1, n // 2):
        before, after = shift(before, 1), shift(after, -1)
        whole = put(whole, before, me + n - step)
        whole = put(whole, after, me + step)
    half = block.shape[0] // 2
    whole = put(whole, shift(before[:half], 1), me + n // 2)
    return put(whole, shift(after[half:], -1), me + n // 2, half)


def gather_plane(block):
    return spread(block, PLANE).reshape(lax.axis_size("ylo"), -1, block.shape[1])


def gather_line(block):
    line = spread(block, "z")
    return line.reshape(line.shape[0] * line.shape[1], line.shape[2])


def reduce_blocks(inputs, other_inputs, adjoint):
    half = adjoint.shape[1] // 2

    def outer(part, rows):
        return lax.dot_general(
            part, rows, (((0,), (0,)), ((), ())), preferred_element_type=jnp.float32
        )

    swapped = core_swap(adjoint[:, half:])
    chip = outer(adjoint[:, :half], inputs) + outer(swapped, other_inputs)
    chip = chip.astype(jnp.bfloat16)
    n_low, n_plane, n_line = lax.axis_size("ylo"), lax.axis_size(PLANE), lax.axis_size("z")
    cols = half // n_low
    blocks = chip.reshape(n_low, cols, n_plane // n_low, -1).transpose(0, 2, 1, 3)
    parts = exchange(blocks.reshape(n_plane, cols, -1), PLANE)
    line = jnp.sum(parts.astype(jnp.float32), axis=0).astype(jnp.bfloat16)
    line = line.reshape(cols, n_line, -1).transpose(1, 2, 0)
    return jnp.sum(exchange(line, "z").astype(jnp.float32), axis=0)


def norm_jacobian(vector, unit_values, root_mean):
    inner = jnp.mean(unit_values * vector, axis=-1, keepdims=True)
    return (vector - unit_values * inner) / root_mean


def turn_rows(text_mask, turn_ids, cols):
    flat = jnp.concatenate([turn_ids.astype(jnp.float32), text_mask]).astype(jnp.bfloat16)
    return jnp.pad(flat, (0, -flat.shape[0] % (16 * cols))).reshape(-1, cols)


def turn_counts(text_mask, turn_ids, before, after):
    n = turn_ids.shape[0]
    turns = turn_ids.astype(jnp.float32)
    counts = jnp.sum(jnp.where(turns[:, None] == turns[None, :], text_mask[None, :], 0.0), axis=1)
    for rows, there in (before, after):
        flat = rows.astype(jnp.float32).reshape(-1)
        same = (turns[:, None] == flat[None, :n]) & there
        counts = counts + jnp.sum(jnp.where(same, flat[None, n : 2 * n], 0.0), axis=1)
    return counts


def local(acts, token_ids, turn_ids, value_weight, norm_gain, query_grad):
    inputs = acts.reshape(acts.shape[1], acts.shape[2])
    ids = turn_ids.reshape(-1)
    features = value_weight.shape[1]
    n_group = lax.axis_size(GROUP)
    turn_total = TURN_DEV * lax.axis_size(SHARD) * n_group
    cols = features // n_group
    me = lax.axis_index(GROUP)
    core = lax.axis_index("core")
    text_mask = (token_ids.reshape(-1) < first_special).astype(jnp.float32)

    def own(array):
        return lax.dynamic_slice(array, (0, me * cols), (array.shape[0], cols))

    other_inputs = core_swap(inputs)

    def project(mine, other_inputs=other_inputs):
        half = jnp.concatenate([mine[0], mine[1]], axis=1)
        swapped = core_swap(jnp.dot(other_inputs, half, preferred_element_type=jnp.float32))
        own_part = jnp.dot(inputs, half, preferred_element_type=jnp.float32)
        return jnp.concatenate([own_part, swapped], axis=1)

    gain = norm_gain.reshape(2, 2, cols)
    gain = jnp.concatenate(
        [jnp.where(core == 0, gain[:, 0], gain[:, 1]), jnp.where(core == 0, gain[:, 1], gain[:, 0])]
    ).reshape(-1)
    gain_square = gain * gain
    query = own(query_grad)

    n_z = lax.axis_size("z")
    tokens = turn_rows(text_mask, ids, cols)
    count = tokens.shape[0]
    rows = value_weight.shape[0]
    line = spread(jnp.concatenate([own(value_weight), tokens]), "z")
    line, tokens = line[:, :rows].reshape(-1, cols), line[:, rows:]
    block = jnp.concatenate([query.astype(jnp.bfloat16), tokens[0], tokens[n_z - 1]])
    block, line = lax.optimization_barrier((block, line))
    plane = spread(block, PLANE)
    plane, line = lax.optimization_barrier((plane, line))
    plane, ends = plane[:, :rows], plane[:, rows:]
    place, chain = lax.axis_index("z"), lax.axis_index(("yhi", "x"))
    n_chain = lax.axis_size(("yhi", "x"))
    base = lax.axis_index("ylo") * n_chain

    def pick(array, index):
        return lax.dynamic_index_in_dim(array, index, keepdims=False)

    before = jnp.where(
        place > 0,
        pick(tokens, jnp.maximum(place - 1, 0)),
        pick(ends, base + jnp.maximum(chain - 1, 0))[count:],
    )
    after = jnp.where(
        place < n_z - 1,
        pick(tokens, jnp.minimum(place + 1, n_z - 1)),
        pick(ends, base + jnp.minimum(chain + 1, n_chain - 1))[:count],
    )
    before = (before, (place > 0) | (chain > 0))
    after = (after, (place < n_z - 1) | (chain < n_chain - 1))
    tangent = project(ring_gather(plane).reshape(lax.axis_size("ylo"), -1, cols))
    values = project(gather_plane(line))
    own_count = turn_counts(text_mask, ids, before, after)
    turn_weight = text_mask / (jnp.maximum(own_count, 1.0) * jnp.float32(turn_total))
    root_mean = jnp.sqrt(jnp.mean(values * values, axis=-1, keepdims=True) + 1e-06)
    unit_values = values / root_mean
    estimate = query
    for step in range(ITERS):
        if step:
            line = gather_line(estimate.astype(jnp.bfloat16))
            line, acts_now = lax.optimization_barrier((line, inputs))
            other_inputs = core_swap(acts_now)
            tangent = project(gather_plane(line), other_inputs)
        inner = gain_square * norm_jacobian(tangent, unit_values, root_mean)
        adjoint = (turn_weight[:, None] * norm_jacobian(inner, unit_values, root_mean)).astype(
            jnp.bfloat16
        )
        curvature = reduce_blocks(inputs, other_inputs, adjoint)
        estimate = query + estimate - (curvature + damping * estimate) / lissa_scale
    whole = spread(estimate, GROUP)
    return jnp.concatenate([whole[i] for i in range(n_group)], axis=1)


def solution(mesh):
    fine = Mesh(mesh.devices.reshape(2, 2, 2, 4, 8), FINE)
    placed = (
        P(GROUP, SHARD, None),
        P(GROUP, SHARD),
        P(GROUP, SHARD),
        P(SHARD, None),
        P(),
        P(SHARD, None),
    )
    return jax.shard_map(
        local, mesh=fine, in_specs=placed, out_specs=P(SHARD, None), check_vma=False
    )
```

```python
import jax
import jax.numpy as jnp
from jax import lax
from jax.sharding import Mesh, PartitionSpec as P

TURN_DEV = 4
ITERS = 2

damping = 1.0
lissa_scale = 12.0
first_special = 128000

FINE = ("ylo", "core", "yhi", "x", "z")
GROUP = ("ylo", "core")
SHARD = ("yhi", "x", "z")
PLANE = ("ylo", "yhi", "x")


def core_swap(value):
    return lax.ppermute(value, "core", [(0, 1), (1, 0)])


def exchange(blocks, axes):
    return lax.all_to_all(blocks, axes, split_axis=0, concat_axis=0, tiled=True)


def spread(block, axes):
    n = lax.axis_size(axes)
    return exchange(jnp.broadcast_to(block[None], (n,) + block.shape), axes)


def ring_gather(block):
    n = lax.axis_size("z")
    me = lax.axis_index("z")
    whole = jnp.zeros((block.shape[0], n) + block.shape[1:], block.dtype)

    def shift(value, step):
        return lax.ppermute(value, "z", [(i, (i + step) % n) for i in range(n)])

    def put(whole, piece, owner, start=0):
        return lax.dynamic_update_slice(whole, piece[:, None], (start, owner % n, 0, 0))

    whole = put(whole, block, me)
    before = after = block
    for step in range(1, n // 2):
        before, after = shift(before, 1), shift(after, -1)
        whole = put(whole, before, me + n - step)
        whole = put(whole, after, me + step)
    half = block.shape[0] // 2
    whole = put(whole, shift(before[:half], 1), me + n // 2)
    return put(whole, shift(after[half:], -1), me + n // 2, half)


def gather_plane(block):
    return spread(block, PLANE).reshape(lax.axis_size("ylo"), -1, block.shape[1])


def gather_line(block):
    line = spread(block, "z")
    return line.reshape(line.shape[0] * line.shape[1], line.shape[2])


def reduce_blocks(inputs, other_inputs, adjoint):
    half = adjoint.shape[1] // 2

    def outer(part, rows):
        return lax.dot_general(
            part, rows, (((0,), (0,)), ((), ())), preferred_element_type=jnp.float32
        )

    swapped = core_swap(adjoint[:, half:])
    chip = outer(adjoint[:, :half], inputs) + outer(swapped, other_inputs)
    chip = chip.astype(jnp.bfloat16)
    n_low, n_plane, n_line = lax.axis_size("ylo"), lax.axis_size(PLANE), lax.axis_size("z")
    cols = half // n_low
    blocks = chip.reshape(n_low, cols, n_plane // n_low, -1).transpose(0, 2, 1, 3)
    parts = exchange(blocks.reshape(n_plane, cols, -1), PLANE)
    line = jnp.sum(parts.astype(jnp.float32), axis=0).astype(jnp.bfloat16)
    line = line.reshape(cols, n_line, -1).transpose(1, 2, 0)
    return jnp.sum(exchange(line, "z").astype(jnp.float32), axis=0)


def norm_jacobian(vector, unit_values, root_mean):
    inner = jnp.mean(unit_values * vector, axis=-1, keepdims=True)
    return (vector - unit_values * inner) / root_mean


def turn_rows(text_mask, turn_ids, cols):
    flat = jnp.concatenate([turn_ids.astype(jnp.float32), text_mask]).astype(jnp.bfloat16)
    return jnp.pad(flat, (0, -flat.shape[0] % (16 * cols))).reshape(-1, cols)


def turn_counts(text_mask, turn_ids, before, after):
    n = turn_ids.shape[0]
    turns = turn_ids.astype(jnp.float32)
    counts = jnp.sum(jnp.where(turns[:, None] == turns[None, :], text_mask[None, :], 0.0), axis=1)
    for rows, there in (before, after):
        flat = rows.astype(jnp.float32).reshape(-1)
        same = (turns[:, None] == flat[None, :n]) & there
        counts = counts + jnp.sum(jnp.where(same, flat[None, n : 2 * n], 0.0), axis=1)
    return counts


def local(acts, token_ids, turn_ids, value_weight, norm_gain, query_grad):
    inputs = acts.reshape(acts.shape[1], acts.shape[2])
    ids = turn_ids.reshape(-1)
    features = value_weight.shape[1]
    n_group = lax.axis_size(GROUP)
    turn_total = TURN_DEV * lax.axis_size(SHARD) * n_group
    cols = features // n_group
    me = lax.axis_index(GROUP)
    core = lax.axis_index("core")
    text_mask = (token_ids.reshape(-1) < first_special).astype(jnp.float32)

    def own(array):
        return lax.dynamic_slice(array, (0, me * cols), (array.shape[0], cols))

    other_inputs = core_swap(inputs)

    def project(mine, other_inputs=other_inputs):
        half = jnp.concatenate([mine[0], mine[1]], axis=1)
        swapped = core_swap(jnp.dot(other_inputs, half, preferred_element_type=jnp.float32))
        own_part = jnp.dot(inputs, half, preferred_element_type=jnp.float32)
        return jnp.concatenate([own_part, swapped], axis=1)

    gain = norm_gain.reshape(2, 2, cols)
    gain = jnp.concatenate(
        [jnp.where(core == 0, gain[:, 0], gain[:, 1]), jnp.where(core == 0, gain[:, 1], gain[:, 0])]
    ).reshape(-1)
    gain_square = gain * gain
    query = own(query_grad)

    n_z = lax.axis_size("z")
    tokens = turn_rows(text_mask, ids, cols)
    count = tokens.shape[0]
    rows = value_weight.shape[0]
    line = spread(jnp.concatenate([own(value_weight), tokens]), "z")
    line, tokens = line[:, :rows].reshape(-1, cols), line[:, rows:]
    block = jnp.concatenate([query.astype(jnp.bfloat16), tokens[0], tokens[n_z - 1]])
    block, line = lax.optimization_barrier((block, line))
    plane = spread(block, PLANE)
    plane, line = lax.optimization_barrier((plane, line))
    plane, ends = plane[:, :rows], plane[:, rows:]
    place, chain = lax.axis_index("z"), lax.axis_index(("yhi", "x"))
    n_chain = lax.axis_size(("yhi", "x"))
    base = lax.axis_index("ylo") * n_chain

    def pick(array, index):
        return lax.dynamic_index_in_dim(array, index, keepdims=False)

    before = jnp.where(
        place > 0,
        pick(tokens, jnp.maximum(place - 1, 0)),
        pick(ends, base + jnp.maximum(chain - 1, 0))[count:],
    )
    after = jnp.where(
        place < n_z - 1,
        pick(tokens, jnp.minimum(place + 1, n_z - 1)),
        pick(ends, base + jnp.minimum(chain + 1, n_chain - 1))[:count],
    )
    before = (before, (place > 0) | (chain > 0))
    after = (after, (place < n_z - 1) | (chain < n_chain - 1))
    tangent = project(ring_gather(plane).reshape(lax.axis_size("ylo"), -1, cols))
    values = project(gather_plane(line))
    own_count = turn_counts(text_mask, ids, before, after)
    turn_weight = text_mask / (jnp.maximum(own_count, 1.0) * jnp.float32(turn_total))
    root_mean = jnp.sqrt(jnp.mean(values * values, axis=-1, keepdims=True) + 1e-06)
    unit_values = values / root_mean
    estimate = query
    for step in range(ITERS):
        if step:
            block, acts_now = lax.optimization_barrier((estimate.astype(jnp.bfloat16), inputs))
            line, other_inputs = lax.optimization_barrier(
                (gather_line(block), core_swap(acts_now))
            )
            tangent = project(gather_plane(line), other_inputs)
        inner = gain_square * norm_jacobian(tangent, unit_values, root_mean)
        adjoint = (turn_weight[:, None] * norm_jacobian(inner, unit_values, root_mean)).astype(
            jnp.bfloat16
        )
        curvature = reduce_blocks(inputs, other_inputs, adjoint)
        estimate = query + estimate - (curvature + damping * estimate) / lissa_scale
    whole = spread(estimate, GROUP)
    return jnp.concatenate([whole[i] for i in range(n_group)], axis=1)


def solution(mesh):
    fine = Mesh(mesh.devices.reshape(2, 2, 2, 4, 8), FINE)
    placed = (
        P(GROUP, SHARD, None),
        P(GROUP, SHARD),
        P(GROUP, SHARD),
        P(SHARD, None),
        P(),
        P(SHARD, None),
    )
    return jax.shard_map(
        local, mesh=fine, in_specs=placed, out_specs=P(SHARD, None), check_vma=False
    )
```
